256 devices in a mesh: seq: 64 (over z, y, core), hid: 4 (over x).
Axes of the slice: x: 4, y: 4, z: 8, core: 2. Of those that a mesh axis runs over, the one named last changes fastest.
Arguments:
- tokens: bfloat16 [65536, 768], P('seq', 'hid'), may hold values from -6 to 6
- first_gain: float32 [768], P('hid'), may hold values from 0.25 to 1.75
- first_shift: float32 [768], P('hid'), may hold values from -3 to 3
- inner_weight: bfloat16 [768, 3072], P(None, 'hid'), may hold values from -0.21875 to 0.21875
- inner_bias: float32 [3072], P('hid'), may hold values from -3 to 3
- outer_weight: bfloat16 [3072, 768], P('hid'), may hold values from -0.109375 to 0.109375
- outer_bias: float32 [768], P('hid'), may hold values from -3 to 3
- second_gain: float32 [768], P('hid'), may hold values from 0.25 to 1.75
- second_shift: float32 [768], P('hid'), may hold values from -3 to 3
Outputs:
- encoded: bfloat16 [65536, 768], P('seq', 'hid')
The draws below stay inside these ranges and needn't reach their ends.
All inputs are finite; a program needn't handle non-finite values.
Results may differ from the reference program's by a relative error of at most 0.0051.
Values may be sent and summed in bfloat16 or wider, within the bound.
No kernel may reach another device: no remote copies, remote signals or barrier semaphores. Data moves between devices by JAX's collectives and lax.ppermute only.
A program may use at most 64 MiB of HBM per device.

```python
import math
import jax
import jax.numpy as jnp
from jax import lax

D = 768
FF = 3072
SEQ = 65536


def block_levels(key, shape, split, least, top_value):
    loudness = 1.0
    for axis_at, shards_of in split:
        steps = jax.random.uniform(jax.random.fold_in(jax.random.fold_in(key, 6), axis_at), (shards_of,), jnp.float32, least / len(split), top_value / len(split))
        loudness = loudness * jnp.repeat(jnp.exp(steps), shape[axis_at] // shards_of).reshape((-1,) + (1,) * (len(shape) - 1 - axis_at))
    return loudness


def normal_values(key, dims, scale, bound, cuts=(), held_as=jnp.bfloat16):
    result = scale * jax.random.normal(key, dims, jnp.float32)
    if cuts:
        result = result * block_levels(key, dims, cuts, -0.22, 0.18)
    return jnp.clip(result, -bound, bound).astype(held_as)


def setup_inputs(seed: int = 0) -> dict:
    arg_keys = jax.random.split(jax.random.key(seed), 10)
    return {
        "tokens": normal_values(arg_keys[0], (SEQ, D), 1.0, 6.0, ((0, 64), (1, 4))),
        "first_gain": jnp.clip(1.0 + 0.15 * jax.random.normal(arg_keys[1], (D,), jnp.float32), 0.25, 1.75),
        "first_shift": normal_values(arg_keys[2], (D,), 0.5, 3.0, ((0, 4),), jnp.float32),
        "inner_weight": normal_values(arg_keys[3], (D, FF), D ** -0.5, 0.21875, ((1, 4),)),
        "inner_bias": normal_values(arg_keys[4], (FF,), 0.5, 3.0, ((0, 4),), jnp.float32),
        "outer_weight": normal_values(arg_keys[5], (FF, D), FF ** -0.5, 0.109375, ((0, 4),)),
        "outer_bias": normal_values(arg_keys[6], (D,), 0.5, 3.0, ((0, 4),), jnp.float32),
        "second_gain": jnp.clip(1.0 + 0.15 * jax.random.normal(arg_keys[7], (D,), jnp.float32), 0.25, 1.75),
        "second_shift": normal_values(arg_keys[8], (D,), 0.5, 3.0, ((0, 4),), jnp.float32),
    }


def hidden_tables(width, first, count):
    rows = jnp.arange(width, dtype=jnp.int32)[:, None]
    columns = first + jnp.arange(count, dtype=jnp.int32)[None, :]
    phase = rows * columns % width
    angle = 2.0 * math.pi / width * phase.astype(jnp.float32)
    return (jnp.cos(angle).astype(jnp.bfloat16), (-jnp.sin(angle)).astype(jnp.bfloat16))

def layer_norm(values, gain, shift):
    mean = lax.optimization_barrier(jnp.mean(values, axis=1, keepdims=True))
    spread = lax.optimization_barrier(jnp.mean(values * values, axis=1, keepdims=True)) - mean * mean
    return (values - mean) * lax.rsqrt(spread + 1e-05) * gain + shift

def reference(tokens, first_gain, first_shift, inner_weight, inner_bias, outer_weight, outer_bias, second_gain, second_shift):
    total = tokens.shape[0]
    width = tokens.shape[1]
    cos_table, sin_table = hidden_tables(width, 0, width)
    column_block = math.gcd(width, 64)
    scale = 1.0 / math.sqrt(total * width)

    def transform_columns(index):
        start = (index * column_block).astype(jnp.int32)
        cos_part = lax.dynamic_slice_in_dim(cos_table, start, column_block, 1)
        sin_part = lax.dynamic_slice_in_dim(sin_table, start, column_block, 1)
        feature_real = jnp.dot(tokens, cos_part, preferred_element_type=jnp.float32)
        feature_imag = jnp.dot(tokens, sin_part, preferred_element_type=jnp.float32)
        spectrum = jnp.fft.fft(lax.complex(feature_real, feature_imag), axis=0)
        return jnp.real(spectrum)
    blocks = lax.map(transform_columns, jnp.arange(width // column_block, dtype=jnp.int32))
    mixed = jnp.transpose(blocks, (1, 0, 2)).reshape(total, width) * scale
    row_block = math.gcd(total, 4096)

    def finish_rows(index):
        start = (index * row_block).astype(jnp.int32)
        token_rows = lax.dynamic_slice_in_dim(tokens, start, row_block, 0)
        mixed_rows = lax.dynamic_slice_in_dim(mixed, start, row_block, 0)
        first_sum = token_rows.astype(jnp.float32) + mixed_rows
        normed = layer_norm(first_sum, first_gain, first_shift).astype(jnp.bfloat16)
        inner = jnp.dot(normed, inner_weight, preferred_element_type=jnp.float32) + inner_bias
        active = jax.nn.gelu(inner, approximate=True).astype(jnp.bfloat16)
        outer = jnp.dot(active, outer_weight, preferred_element_type=jnp.float32)
        second_sum = normed.astype(jnp.float32) + outer + outer_bias
        return layer_norm(second_sum, second_gain, second_shift).astype(jnp.bfloat16)
    finished = lax.map(finish_rows, jnp.arange(total // row_block, dtype=jnp.int32))
    return finished.reshape(total, width)
```

```python
import math

import jax
import jax.numpy as jnp
import ml_dtypes
import numpy as np
from jax import lax
from jax.sharding import PartitionSpec as P

D = 768
HALF = D // 2
SEQ = 65536
R = 256
SEQ_DEVICES = 64
HID_DEVICES = 4
WIDTH = D // HID_DEVICES
EVERY = ("hid", "seq")
BF16 = ml_dtypes.bfloat16


def residues():
    place = np.arange(R)
    hid, seq = place // SEQ_DEVICES, place % SEQ_DEVICES
    chip = (seq >> 1) * HID_DEVICES + hid
    core = seq & 1
    return np.where(core == 0, chip, np.where(chip == 0, R // 2, R - chip)), chip, core


RESIDUE, CHIP, CORE = residues()
ROW = np.arange(R)
HIGH = HID_DEVICES * (ROW % SEQ_DEVICES) + ROW // SEQ_DEVICES


def cosine_sine(phase, period):
    angle = 2.0 * np.pi * (phase % period).astype(np.float64) / period
    return np.cos(angle), np.sin(angle)


def feature_table():
    rows = np.arange(D, dtype=np.int64)[:, None]
    columns = np.arange(HALF + 1, dtype=np.int64)[None, :]
    angle = np.float32(2.0 * math.pi / D) * (rows * columns % D).astype(np.float32)
    cosine = np.cos(angle.astype(np.float64)).astype(BF16)
    sine = (-np.sin(angle.astype(np.float64))).astype(BF16)
    sine[:, 0] = cosine[:, HALF]
    return np.concatenate([cosine[:, :HALF], sine[:, :HALF]], axis=1)


def make_tables():
    spread = (RESIDUE[:, None] == ROW[None, :]).astype(BF16)
    first_cos, first_sin = cosine_sine(RESIDUE[:, None] * HIGH[None, :], R)
    first = np.concatenate([first_cos, first_sin]).astype(BF16)
    base_cos, base_sin = cosine_sine(HIGH[:, None] * RESIDUE[None, :], R)
    base = np.stack([base_cos, base_sin]).astype(np.float32)
    own = cosine_sine(RESIDUE[:, None] * RESIDUE[None, :], SEQ)
    opposite = (R - RESIDUE) % R
    other = cosine_sine(opposite[:, None] * RESIDUE[None, :], SEQ)
    turn = np.stack([*own, *other], axis=1).astype(np.float32)
    lane = np.arange(HALF)
    mirror = (lane[:, None] == (HALF - lane[None, :]) % HALF).astype(BF16)
    return spread, first, base, turn, mirror


FEATURE = feature_table()
SPREAD, FIRST, BASE, TURN, MIRROR = make_tables()


def norm_rows(values, gain, shift):
    mean = jnp.mean(values, axis=1, keepdims=True)
    spread = jnp.mean(values * values, axis=1, keepdims=True) - mean * mean
    return (values - mean) * lax.rsqrt(spread + 1e-05) * gain + shift


def dot(left, right):
    return jnp.dot(left, right, preferred_element_type=jnp.float32)


def pair_index(seq, hid):
    return seq * HID_DEVICES + hid % HID_DEVICES


def ring(value, sign):
    pairs = []
    for seq in range(SEQ_DEVICES):
        step = -sign if seq & 1 else sign
        for hid in range(HID_DEVICES):
            pairs.append((pair_index(seq, hid), pair_index(seq, hid + step)))
    return lax.ppermute(value, ("seq", "hid"), pairs)


def swap_cores(value):
    return lax.ppermute(value, "seq", [(seq, seq ^ 1) for seq in range(SEQ_DEVICES)])


def swap_mirrored(value):
    pairs = []
    for seq in range(SEQ_DEVICES):
        for hid in range(HID_DEVICES):
            alone = seq < 2 and hid == 0
            pairs.append((pair_index(seq, hid), pair_index(seq if alone else seq ^ 1, hid)))
    return lax.ppermute(value, ("seq", "hid"), pairs)


def shift_hid(value, step):
    pairs = [(hid, (hid + step) % HID_DEVICES) for hid in range(HID_DEVICES)]
    return lax.ppermute(value, "hid", pairs)


def shards(
    tokens,
    first_gain,
    first_shift,
    inner_weight,
    inner_bias,
    outer_weight,
    outer_bias,
    second_gain,
    second_shift,
):
    bf16 = jnp.bfloat16
    f32 = jnp.float32
    seq = lax.axis_index("seq")
    hid = lax.axis_index("hid")
    core = seq & 1
    place = hid * SEQ_DEVICES + seq
    alone = place < 2

    hidden = inner_weight.shape[1]
    part = hidden // 2
    inner_half = lax.dynamic_slice_in_dim(inner_weight, core * part, part, 1)
    outer_half = lax.dynamic_slice_in_dim(outer_weight, core * part, part, 0)
    payload = jnp.concatenate([inner_half, outer_half[:, :HALF], outer_half[:, HALF:]], axis=0)
    ring_one = ring(payload, 1)
    ring_three = ring(payload, -1)
    ring_two = ring(ring_one, 1)
    others = [ring_one, ring_two, ring_three]
    others = others + [swap_cores(each) for each in others]
    small = jnp.concatenate(
        [
            first_gain[None],
            first_shift[None],
            outer_bias[None],
            second_gain[None],
            second_shift[None],
            inner_bias.reshape(HID_DEVICES, WIDTH),
        ]
    )
    around = [small, shift_hid(small, -1), shift_hid(small, 2), shift_hid(small, 1)]
    around = jnp.stack(around + around)
    vectors = lax.dynamic_slice_in_dim(around, (HID_DEVICES - hid) % HID_DEVICES, HID_DEVICES, 0)
    rows = jnp.transpose(vectors[:, :5], (1, 0, 2)).reshape(5, 1, D)
    biases = vectors[:, 5:].reshape(HID_DEVICES * 2, part)
    sign = 1 - 2 * core

    def bias_of(shard, half):
        index = (shard + HID_DEVICES) % HID_DEVICES * 2 + half
        return lax.dynamic_slice_in_dim(biases, index, 1, 0)

    other_biases = [
        bias_of(hid - sign, core),
        bias_of(hid + 2, core),
        bias_of(hid + sign, core),
        bias_of(hid + sign, 1 - core),
        bias_of(hid + 2, 1 - core),
        bias_of(hid - sign, 1 - core),
    ]

    blocks = tokens.reshape(HID_DEVICES, R, WIDTH)
    sent = jnp.einsum("dm,amc->dac", jnp.asarray(SPREAD), blocks, preferred_element_type=f32)
    sent = sent.astype(bf16).reshape(R, D)
    taken = lax.all_to_all(sent, EVERY, 0, 0, tiled=True)
    local = taken.reshape(HID_DEVICES, SEQ_DEVICES, HID_DEVICES, WIDTH)
    local = jnp.transpose(local, (2, 1, 0, 3)).reshape(R, D)

    features = dot(local, jnp.asarray(FEATURE)).astype(bf16)
    turned = dot(jnp.asarray(FIRST), features)
    cos_real, cos_imag = turned[:R, :HALF], turned[:R, HALF:]
    sin_real, sin_imag = turned[R:, :HALF], turned[R:, HALF:]
    lane = lax.broadcasted_iota(jnp.int32, (R, HALF), 1)
    row_core = jnp.asarray(CORE.astype(np.int32))[:, None]
    row_alone = jnp.asarray((CHIP == 0))[:, None]
    edge = lane == 0
    late = jnp.logical_and(row_core == 1, jnp.logical_not(row_alone))
    edge_real = jnp.where(late, cos_imag, cos_real)
    edge_imag = jnp.where(row_alone, cos_imag, -jnp.where(late, sin_imag, sin_real))
    spectrum_real = jnp.where(edge, edge_real, cos_real + sin_imag)
    spectrum_imag = jnp.where(edge, edge_imag, cos_imag - sin_real)
    sent = jnp.concatenate([spectrum_real, spectrum_imag], axis=1).astype(bf16)
    taken = lax.all_to_all(sent, EVERY, 0, 0, tiled=True)

    turn = lax.dynamic_slice_in_dim(jnp.asarray(TURN), place, 1, 0)[0]
    base_cos, base_sin = jnp.asarray(BASE[0]), jnp.asarray(BASE[1])
    own_cos = base_cos * turn[0] - base_sin * turn[1]
    own_sin = base_sin * turn[0] + base_cos * turn[1]
    other_cos = base_cos * turn[2] - base_sin * turn[3]
    other_sin = base_sin * turn[2] + base_cos * turn[3]
    real, imag = taken[:, :HALF], taken[:, HALF:]
    single = jnp.logical_and(edge, alone)
    zero = jnp.zeros((), bf16)
    imag_cut = jnp.where(single, zero, imag)
    real_cut = jnp.where(single, imag, real)
    own = dot(own_cos.astype(bf16), real) + dot(own_sin.astype(bf16), imag_cut)
    opposite = dot(other_cos.astype(bf16), real_cut) - dot(other_sin.astype(bf16), imag_cut)
    scale = 1.0 / math.sqrt(SEQ * D)
    received = swap_mirrored((opposite * scale).astype(bf16))
    own = own * scale
    crossed = jnp.logical_and(edge, jnp.logical_and(core == 1, jnp.logical_not(alone)))
    low = jnp.where(crossed, received.astype(f32), own)
    high = jnp.where(crossed, own, received.astype(f32)).astype(bf16)
    mixed = jnp.concatenate([low, dot(high, jnp.asarray(MIRROR))], axis=1)

    first_sum = local.astype(f32) + mixed
    normed = norm_rows(first_sum, rows[0], rows[1]).astype(bf16)

    inner = dot(normed, inner_weight) + inner_bias
    active = jax.nn.gelu(inner, approximate=True).astype(bf16)
    outer = dot(active, outer_weight)
    for each, bias in zip(others, other_biases):
        inner = dot(normed, each[:D]) + bias
        active = jax.nn.gelu(inner, approximate=True).astype(bf16)
        outer = outer + jnp.concatenate(
            [dot(active, each[D : D + part]), dot(active, each[D + part :])], axis=1
        )
    second_sum = normed.astype(f32) + outer + rows[2]
    finished = norm_rows(second_sum, rows[3], rows[4]).astype(bf16)

    sent = finished.reshape(HID_DEVICES, SEQ_DEVICES, HID_DEVICES, WIDTH)
    sent = jnp.transpose(sent, (2, 1, 0, 3)).reshape(R, D)
    taken = lax.all_to_all(sent, EVERY, 0, 0, tiled=True)
    ordered = jnp.einsum(
        "dm,dac->amc",
        jnp.asarray(SPREAD),
        taken.reshape(R, HID_DEVICES, WIDTH),
        preferred_element_type=f32,
    )
    return ordered.astype(bf16).reshape(tokens.shape)


def solution(mesh):
    return jax.shard_map(
        shards,
        mesh=mesh,
        in_specs=(
            P("seq", "hid"),
            P("hid"),
            P("hid"),
            P(None, "hid"),
            P("hid"),
            P("hid", None),
            P("hid"),
            P("hid"),
            P("hid"),
        ),
        out_specs=P("seq", "hid"),
        check_vma=False,
    )
```

```python
import math

import jax
import jax.numpy as jnp
import ml_dtypes
import numpy as np
from jax import lax
from jax.experimental import pallas as pl
from jax.experimental.pallas import tpu as pltpu
from jax.sharding import PartitionSpec as P

D = 768
HALF = D // 2
SEQ = 65536
R = 256
SEQ_DEVICES = 64
HID_DEVICES = 4
WIDTH = D // HID_DEVICES
EVERY = ("hid", "seq")
BF16 = ml_dtypes.bfloat16


def residues():
    place = np.arange(R)
    hid, seq = place // SEQ_DEVICES, place % SEQ_DEVICES
    chip = (seq >> 1) * HID_DEVICES + hid
    core = seq & 1
    return np.where(core == 0, chip, np.where(chip == 0, R // 2, R - chip)), chip, core


RESIDUE, CHIP, CORE = residues()
ROW = np.arange(R)
HIGH = 4 * (ROW % 128 // 2) + 2 * (ROW % 2) + ROW // 128


def cosine_sine(phase, period):
    angle = 2.0 * np.pi * (phase % period).astype(np.float64) / period
    return np.cos(angle), np.sin(angle)


def feature_table():
    rows = np.arange(D, dtype=np.int64)[:, None]
    columns = np.arange(HALF + 1, dtype=np.int64)[None, :]
    angle = np.float32(2.0 * math.pi / D) * (rows * columns % D).astype(np.float32)
    cosine = np.cos(angle.astype(np.float64)).astype(BF16)
    sine = (-np.sin(angle.astype(np.float64))).astype(BF16)
    sine[:, 0] = cosine[:, HALF]
    return np.concatenate([cosine[:, :HALF], sine[:, :HALF]], axis=1)


def pairs_of_rows(even, odd):
    return np.stack([even, odd], axis=1).reshape(2 * even.shape[0], -1)


def high_table():
    cosine, sine = cosine_sine(RESIDUE[:, None] * HIGH[None, :], R)
    even = np.concatenate([cosine, sine], axis=1)
    odd = np.concatenate([-sine, cosine], axis=1)
    return pairs_of_rows(even, odd).astype(BF16)


def low_tables():
    cosine, sine = cosine_sine(HIGH[:, None] * RESIDUE[None, :], R)
    table = np.stack([pairs_of_rows(cosine.T, sine.T).T, pairs_of_rows(-sine.T, cosine.T).T])
    own = cosine_sine(RESIDUE[:, None] * RESIDUE[None, :], SEQ)
    other = cosine_sine((R - RESIDUE)[:, None] % R * RESIDUE[None, :], SEQ)
    sign = np.where(np.arange(2 * R) % 2 == 0, 1.0, -1.0)
    turn = [np.repeat(each, 2, axis=1) for each in own]
    turn += [np.repeat(each, 2, axis=1) * sign for each in other]
    return table.astype(np.float32), np.stack(turn, axis=1).astype(np.float32)


FEATURE = feature_table()
HIGH_TABLE = high_table()
LOW_TABLE, LOW_TURN = low_tables()
LANE = np.arange(HALF)
MIRROR = (LANE[:, None] == (HALF - LANE[None, :]) % HALF).astype(BF16)


def dot(left, right):
    return jnp.dot(left, right, preferred_element_type=jnp.float32)


def norm_rows(values, gain, shift):
    mean = jnp.mean(values, axis=1, keepdims=True)
    spread = jnp.mean(values * values, axis=1, keepdims=True) - mean * mean
    return (values - mean) * lax.rsqrt(spread + 1e-05) * gain + shift


def residue_of(place):
    hid, seq = place // SEQ_DEVICES, place % SEQ_DEVICES
    chip = seq // 2 * HID_DEVICES + hid
    late = jnp.where(chip == 0, R // 2, R - chip)
    return jnp.where(seq % 2 == 0, chip, late)


def spread_matrix():
    pair = lax.broadcasted_iota(jnp.int32, (2 * R, 1), 0)
    target = pair % 2 * R + residue_of(pair // 2)
    column = lax.broadcasted_iota(jnp.int32, (1, 2 * R), 1)
    return jnp.where(target == column, 1.0, 0.0).astype(jnp.bfloat16)


def scatter_kernel(tokens_ref, out_ref, wide_ref):
    for a in range(4):
        s, u = divmod(a, 2)
        wide_ref[pl.ds(u * WIDTH, WIDTH), pl.ds(s * R, R)] = tokens_ref[:, pl.ds(a * R, R)]
    out_ref[...] = lax.dot_general(
        spread_matrix(),
        wide_ref[...],
        (((1,), (1,)), ((), ())),
        preferred_element_type=jnp.float32,
    ).astype(out_ref.dtype)


def gather_kernel(taken_ref, out_ref):
    ordered = lax.dot_general(
        taken_ref[...],
        spread_matrix(),
        (((0,), (0,)), ((), ())),
        preferred_element_type=jnp.float32,
    ).astype(out_ref.dtype)
    for a in range(4):
        s, u = divmod(a, 2)
        out_ref[:, pl.ds(a * R, R)] = ordered[u * WIDTH : (u + 1) * WIDTH, s * R : (s + 1) * R]


def high_kernel(
    taken_ref, feature_ref, table_ref, kept_ref, out_ref, local_ref, stacked_ref, semaphore
):
    for hid in range(4):
        for u in range(2):
            local_ref[pl.ds(u * 128, 128), pl.ds(hid * WIDTH, WIDTH)] = taken_ref[
                pl.ds(hid * 128, 128), pl.ds(u * WIDTH, WIDTH)
            ]
    keep = pltpu.make_async_copy(local_ref, kept_ref, semaphore)
    keep.start()
    features = dot(local_ref[...], feature_ref[...])
    stacked_ref[pl.ds(0, R), pl.ds(0, HALF)] = features[:, :HALF].astype(jnp.bfloat16)
    stacked_ref[pl.ds(R, R), pl.ds(0, HALF)] = features[:, HALF:].astype(jnp.bfloat16)
    lane = lax.broadcasted_iota(jnp.int32, (R, 128), 1)
    first, middle = features[:, 0:1], features[:, HALF : HALF + 1]
    above = jnp.where(lane == 0, first, jnp.where(lane == 1, middle, 0.0))
    below = jnp.where(lane == 2, middle, 0.0)
    stacked_ref[pl.ds(0, R), pl.ds(HALF, 128)] = above.astype(jnp.bfloat16)
    stacked_ref[pl.ds(R, R), pl.ds(HALF, 128)] = below.astype(jnp.bfloat16)
    turned = dot(table_ref[...], stacked_ref[...])
    pair = lax.broadcasted_iota(jnp.int32, (2 * R, 128), 0)
    lane = lax.broadcasted_iota(jnp.int32, (2 * R, 128), 1)
    place = pair // 2
    alone = place < 2
    edge = turned[:, HALF:]
    single = jnp.where(jnp.logical_and(alone, pair % 2 == 1), edge[:, 2:3], edge[:, 0:1])
    single = jnp.where(jnp.logical_and(~alone, place % 2 == 1), edge[:, 1:2], single)
    out_ref[:, pl.ds(0, 128)] = jnp.where(lane == 0, single, turned[:, :128]).astype(out_ref.dtype)
    out_ref[:, pl.ds(128, HALF - 128)] = turned[:, 128:HALF].astype(out_ref.dtype)
    keep.wait()


def turn_kernel(turns_ref, table_ref, out_ref, turn_ref, semaphore):
    place = lax.axis_index("hid") * SEQ_DEVICES + lax.axis_index("seq")
    copy = pltpu.make_async_copy(turns_ref.at[place], turn_ref, semaphore)
    copy.start()
    copy.wait()
    for index in range(2):
        matrix = (
            table_ref[0] * turn_ref[pl.ds(2 * index, 1), :]
            + table_ref[1] * turn_ref[pl.ds(2 * index + 1, 1), :]
        )
        out_ref[index] = matrix.astype(out_ref.dtype)


def low_kernel(taken_ref, matrix_ref, own_ref, other_ref, wide_ref):
    scale = 1.0 / math.sqrt(SEQ * D)
    alone = jnp.logical_and(lax.axis_index("hid") == 0, lax.axis_index("seq") < 2)
    wide_ref[:, pl.ds(0, HALF)] = taken_ref[...]
    edge = taken_ref[:, pl.ds(0, 128)].astype(jnp.float32)
    row = lax.broadcasted_iota(jnp.int32, (2 * R, 128), 0)
    lane = lax.broadcasted_iota(jnp.int32, (2 * R, 128), 1)
    raised = pltpu.roll(pltpu.roll(edge, 2 * R - 1, 0), 1, 1)
    edge = jnp.where(row % 2 == 0, jnp.where(lane == 0, edge, raised), 0.0)
    wide_ref[:, pl.ds(HALF, 128)] = edge.astype(wide_ref.dtype)
    lane = lax.broadcasted_iota(jnp.int32, (R, 128), 1)
    single = jnp.logical_and(lane == 0, alone)
    for index, out_ref in enumerate((own_ref, other_ref)):
        usual = dot(matrix_ref[index], wide_ref[...]) * scale
        edge = usual[:, HALF + index : HALF + index + 1]
        out_ref[:, pl.ds(0, 128)] = jnp.where(single, edge, usual[:, :128]).astype(out_ref.dtype)
        out_ref[:, pl.ds(128, HALF - 128)] = usual[:, 128:HALF].astype(out_ref.dtype)


def layer_kernel(
    own_any,
    received_any,
    mirror_any,
    local_any,
    small_refs,
    inner_ref,
    outer_ref,
    ring_refs,
    swapped_refs,
    out_ref,
    own_ref,
    received_ref,
    mirror_ref,
    local_ref,
    around_ref,
    weights_ref,
    rows_ref,
    total_ref,
    semaphores,
):
    hid, seq = lax.axis_index("hid"), lax.axis_index("seq")
    core = lax.rem(seq, 2)
    crossed = jnp.logical_and(core == 1, jnp.logical_or(hid > 0, seq >= 2))

    def copy(source, target, index):
        return pltpu.make_async_copy(source, target, semaphores.at[index])

    inputs = [
        copy(received_any, received_ref, 0),
        copy(mirror_any, mirror_ref, 1),
        copy(own_any, own_ref, 2),
        copy(local_any, local_ref, 3),
    ]
    inputs += [copy(each, around_ref.at[at], 4 + at) for at, each in enumerate(small_refs)]
    for each in inputs:
        each.start()
    inner_from = [(inner_ref, inner_ref)] + [(ring_refs[i], swapped_refs[i]) for i in (0, 2, 1)]
    outer_from = [(outer_ref, outer_ref)] + [
        (swapped_refs[j], ring_refs[j]) for j in (2, 0, 1)
    ]
    sources = [each for pair in zip(inner_from, outer_from) for each in pair]

    @pl.when(core == 0)
    def _():
        for index, each in enumerate(sources):
            copy(each[0], weights_ref.at[index], 8 + index).start()

    @pl.when(core == 1)
    def _():
        for index, each in enumerate(sources):
            copy(each[1], weights_ref.at[index], 8 + index).start()

    for each in inputs:
        each.wait()
    for block in range(4):
        at = lax.rem(block - hid + 4, 4)
        rows_ref[:, pl.ds(block * WIDTH, WIDTH)] = around_ref[at][:, :WIDTH]

    received = received_ref[...]
    own = own_ref[...]
    lane = lax.broadcasted_iota(jnp.int32, (R, HALF), 1)
    take = jnp.logical_and(lane == 0, crossed)
    low = jnp.where(take, received.astype(jnp.float32), own)
    high = jnp.where(take, own, dot(received, mirror_ref[...]))
    mixed = jnp.concatenate([low, high], axis=1)
    first_sum = local_ref[...].astype(jnp.float32) + mixed
    normed = norm_rows(first_sum, rows_ref[0:1, :], rows_ref[1:2, :]).astype(jnp.bfloat16)
    total_ref[...] = normed.astype(jnp.float32) + rows_ref[2:3, :]
    for index, distance in enumerate((0, 3, 1, 2)):
        for at in (2 * index, 2 * index + 1):
            copy(sources[at][0], weights_ref.at[at], 8 + at).wait()
        inner = dot(normed, weights_ref[2 * index]) + around_ref[distance, pl.ds(5, 1), :]
        active = jax.nn.gelu(inner, approximate=True).astype(jnp.bfloat16)
        total_ref[...] += dot(active, weights_ref[2 * index + 1])
    finished = norm_rows(total_ref[...], rows_ref[3:4, :], rows_ref[4:5, :]).astype(out_ref.dtype)
    for block in range(4):
        for u in range(2):
            out_ref[pl.ds(block * 128, 128), pl.ds(u * WIDTH, WIDTH)] = finished[
                u * 128 : (u + 1) * 128, block * WIDTH : (block + 1) * WIDTH
            ]


VMEM = pl.BlockSpec(memory_space=pltpu.VMEM)
HBM = pl.BlockSpec(memory_space=pltpu.HBM)
ANYWHERE = pl.BlockSpec(memory_space=pl.ANY)
PARAMS = pltpu.CompilerParams(vmem_limit_bytes=40 * 2**20)


def array(shape, dtype=jnp.bfloat16):
    return jax.ShapeDtypeStruct(shape, dtype)


def pair_index(seq, hid):
    return seq * HID_DEVICES + hid % HID_DEVICES


def ring(value, sign):
    pairs = []
    for seq in range(SEQ_DEVICES):
        step = -sign if seq & 1 else sign
        for hid in range(HID_DEVICES):
            pairs.append((pair_index(seq, hid), pair_index(seq, hid + step)))
    return lax.ppermute(value, ("seq", "hid"), pairs)


def swap_cores(value):
    return lax.ppermute(value, "seq", [(seq, seq ^ 1) for seq in range(SEQ_DEVICES)])


def swap_mirrored(value):
    pairs = []
    for seq in range(SEQ_DEVICES):
        for hid in range(HID_DEVICES):
            alone = seq < 2 and hid == 0
            pairs.append((pair_index(seq, hid), pair_index(seq if alone else seq ^ 1, hid)))
    return lax.ppermute(value, ("seq", "hid"), pairs)


def shift_hid(value, step):
    pairs = [(hid, (hid + step) % HID_DEVICES) for hid in range(HID_DEVICES)]
    return lax.ppermute(value, "hid", pairs)


def shards(
    tokens,
    first_gain,
    first_shift,
    inner_weight,
    inner_bias,
    outer_weight,
    outer_bias,
    second_gain,
    second_shift,
):
    bf16 = jnp.bfloat16
    f32 = jnp.float32
    core = lax.axis_index("seq") & 1

    payload = jnp.where(core == 0, inner_weight, outer_weight)
    ring_one = ring(payload, 1)
    ring_three = ring(payload, -1)

    tokens_t, _ = lax.optimization_barrier((tokens.T, payload))
    sent = pl.pallas_call(
        scatter_kernel,
        out_shape=array((2 * R, HALF)),
        in_specs=[VMEM],
        out_specs=VMEM,
        scratch_shapes=[pltpu.VMEM((HALF, 2 * R), bf16)],
        compiler_params=PARAMS,
    )(tokens_t)
    taken = lax.all_to_all(sent, EVERY, 0, 0, tiled=True)

    vectors = (first_gain, first_shift, outer_bias, second_gain, second_shift)
    vectors, _ = lax.optimization_barrier(((*vectors, inner_bias), sent))
    small = jnp.stack([jnp.pad(each, (0, D - each.shape[0])) for each in vectors])
    small = jnp.concatenate([small, jnp.zeros((2, D), f32)])
    around = [small, shift_hid(small, -1), shift_hid(small, 2), shift_hid(small, 1)]
    taken, _ = lax.optimization_barrier((taken, around))

    local, sent = pl.pallas_call(
        high_kernel,
        out_shape=(array((R, D)), array((2 * R, HALF))),
        in_specs=[VMEM] * 3,
        out_specs=(HBM, VMEM),
        scratch_shapes=[
            pltpu.VMEM((R, D), bf16),
            pltpu.VMEM((2 * R, 2 * R), bf16),
            pltpu.SemaphoreType.DMA,
        ],
        compiler_params=PARAMS,
    )(taken, jnp.asarray(FEATURE), jnp.asarray(HIGH_TABLE))
    taken = lax.all_to_all(sent, EVERY, 0, 0, tiled=True)

    (ring_one, ring_three), _ = lax.optimization_barrier(((ring_one, ring_three), sent))
    ring_two = ring(ring_one, 1)
    swap_one, swap_three = swap_cores(ring_one), swap_cores(ring_three)
    turns, _ = lax.optimization_barrier((jnp.asarray(LOW_TURN), sent))
    matrices = pl.pallas_call(
        turn_kernel,
        out_shape=array((2, R, 2 * R)),
        in_specs=[HBM, VMEM],
        out_specs=VMEM,
        scratch_shapes=[pltpu.VMEM((4, 2 * R), f32), pltpu.SemaphoreType.DMA],
        compiler_params=PARAMS,
    )(turns, jnp.asarray(LOW_TABLE))
    taken, _ = lax.optimization_barrier((taken, matrices))

    own, other = pl.pallas_call(
        low_kernel,
        out_shape=(array((R, HALF), f32), array((R, HALF))),
        in_specs=[VMEM] * 2,
        out_specs=(VMEM, VMEM),
        scratch_shapes=[pltpu.VMEM((2 * R, 2 * R), bf16)],
        compiler_params=PARAMS,
    )(taken, matrices)
    ring_two_there, _ = lax.optimization_barrier((ring_two, taken))
    swap_two = swap_cores(ring_two_there)
    received = swap_mirrored(other)

    def layer(*refs):
        return layer_kernel(*refs[:4], refs[4:8], *refs[8:10], refs[10:13], refs[13:16], *refs[16:])

    sent = pl.pallas_call(
        layer,
        out_shape=array((2 * R, HALF)),
        in_specs=[ANYWHERE] * 16,
        out_specs=VMEM,
        scratch_shapes=[
            pltpu.VMEM((R, HALF), f32),
            pltpu.VMEM((R, HALF), bf16),
            pltpu.VMEM((HALF, HALF), bf16),
            pltpu.VMEM((R, D), bf16),
            pltpu.VMEM((4, 8, D), f32),
            pltpu.VMEM((8, D, D), bf16),
            pltpu.VMEM((8, D), f32),
            pltpu.VMEM((R, D), f32),
            pltpu.SemaphoreType.DMA((16,)),
        ],
        compiler_params=PARAMS,
    )(
        own,
        received,
        jnp.asarray(MIRROR),
        local,
        *around,
        inner_weight,
        outer_weight,
        ring_one,
        ring_two,
        ring_three,
        swap_one,
        swap_two,
        swap_three,
    )
    taken = lax.all_to_all(sent, EVERY, 0, 0, tiled=True)

    return pl.pallas_call(
        gather_kernel,
        out_shape=array(tokens.shape[::-1]),
        in_specs=[VMEM],
        out_specs=VMEM,
        compiler_params=PARAMS,
    )(taken).T


def solution(mesh):
    return jax.shard_map(
        shards,
        mesh=mesh,
        in_specs=(
            P("seq", "hid"),
            P("hid"),
            P("hid"),
            P(None, "hid"),
            P("hid"),
            P("hid", None),
            P("hid"),
            P("hid"),
            P("hid"),
        ),
        out_specs=P("seq", "hid"),
        check_vma=False,
    )
```

```python
import math

import jax
import jax.numpy as jnp
import ml_dtypes
import numpy as np
from jax import lax
from jax.experimental import pallas as pl
from jax.experimental.pallas import tpu as pltpu
from jax.sharding import PartitionSpec as P

D = 768
HALF = D // 2
SEQ = 65536
R = 256
SEQ_DEVICES = 64
HID_DEVICES = 4
WIDTH = D // HID_DEVICES
EVERY = ("hid", "seq")
CHUNKS = (R, 2, HALF)
BF16 = ml_dtypes.bfloat16


def residues():
    place = np.arange(R)
    hid, seq = place // SEQ_DEVICES, place % SEQ_DEVICES
    chip = (seq >> 1) * HID_DEVICES + hid
    core = seq & 1
    return np.where(core == 0, chip, np.where(chip == 0, R // 2, R - chip)), chip, core


RESIDUE, CHIP, CORE = residues()
ROW = np.arange(R)
HIGH = 4 * (ROW % 128 // 2) + 2 * (ROW % 2) + ROW // 128


def cosine_sine(phase, period):
    angle = 2.0 * np.pi * (phase % period).astype(np.float64) / period
    return np.cos(angle), np.sin(angle)


def feature_table():
    rows = np.arange(D, dtype=np.int64)[:, None]
    columns = np.arange(HALF + 1, dtype=np.int64)[None, :]
    angle = np.float32(2.0 * math.pi / D) * (rows * columns % D).astype(np.float32)
    cosine = np.cos(angle.astype(np.float64)).astype(BF16)
    sine = (-np.sin(angle.astype(np.float64))).astype(BF16)
    sine[:, 0] = cosine[:, HALF]
    return np.concatenate([cosine[:, :HALF], sine[:, :HALF]], axis=1)


def pairs_of_rows(even, odd):
    return np.stack([even, odd], axis=1).reshape(2 * even.shape[0], -1)


def high_table():
    cosine, sine = cosine_sine(RESIDUE[:, None] * HIGH[None, :], R)
    even = np.concatenate([cosine, sine], axis=1)
    odd = np.concatenate([-sine, cosine], axis=1)
    return pairs_of_rows(even, odd).astype(BF16)


def low_table():
    cosine, sine = cosine_sine(HIGH[:, None] * RESIDUE[None, :], R)
    table = np.stack([pairs_of_rows(cosine.T, sine.T).T, pairs_of_rows(-sine.T, cosine.T).T])
    return table.astype(np.float32)


FEATURE = feature_table()
HIGH_TABLE = high_table()
LOW_TABLE = low_table()
LANE = np.arange(HALF)
MIRROR = (LANE[:, None] == (HALF - LANE[None, :]) % HALF).astype(BF16)


def dot(left, right):
    return jnp.dot(left, right, preferred_element_type=jnp.float32)


def norm_rows(values, gain, shift):
    mean = jnp.mean(values, axis=1, keepdims=True)
    spread = jnp.mean(values * values, axis=1, keepdims=True) - mean * mean
    return (values - mean) * lax.rsqrt(spread + 1e-05) * gain + shift


def residue_of(place):
    hid, seq = place // SEQ_DEVICES, place % SEQ_DEVICES
    chip = seq // 2 * HID_DEVICES + hid
    late = jnp.where(chip == 0, R // 2, R - chip)
    return jnp.where(seq % 2 == 0, chip, late)


def spread_matrix():
    pair = lax.broadcasted_iota(jnp.int32, (2 * R, 1), 0)
    target = pair % 2 * R + residue_of(pair // 2)
    column = lax.broadcasted_iota(jnp.int32, (1, 2 * R), 1)
    return jnp.where(target == column, 1.0, 0.0).astype(jnp.bfloat16)


def payload_kernel(inner_ref, outer_ref, *rest):
    *vector_refs, payload_ref, rows_ref, semaphore = rest
    core = lax.rem(lax.axis_index("seq"), 2)
    weights = payload_ref.at[pl.ds(0, D)]

    @pl.when(core == 0)
    def _():
        pltpu.make_async_copy(inner_ref, weights, semaphore).start()

    @pl.when(core == 1)
    def _():
        pltpu.make_async_copy(outer_ref, weights, semaphore).start()

    rows_ref[...] = jnp.zeros_like(rows_ref)
    for index, each in enumerate(vector_refs):
        row, at = divmod(index, 4) if index < 5 else (2, 0)
        rows_ref[row : row + 1, pl.ds(at * WIDTH, each.shape[0])] = each[...][None, :]
    rest = rows_ref[...]
    pieces = []
    for _ in range(3):
        pieces.append(rest.astype(jnp.bfloat16).astype(jnp.float32))
        rest = rest - pieces[-1]
    pieces.append(jnp.zeros_like(rest))
    payload_ref[pl.ds(D, EXTRA), :] = jnp.concatenate(pieces, axis=0).astype(jnp.bfloat16)
    pltpu.make_async_copy(inner_ref, weights, semaphore).wait()


def scatter_kernel(tokens_ref, out_ref, wide_ref):
    for a in range(4):
        s, u = divmod(a, 2)
        wide_ref[pl.ds(u * WIDTH, WIDTH), pl.ds(s * R, R)] = tokens_ref[:, pl.ds(a * R, R)]
    spread = lax.dot_general(
        spread_matrix(),
        wide_ref[...],
        (((1,), (1,)), ((), ())),
        preferred_element_type=jnp.float32,
    )
    out_ref[...] = spread.astype(out_ref.dtype).reshape(out_ref.shape)


def gather_kernel(taken_ref, out_ref):
    ordered = lax.dot_general(
        taken_ref[...].reshape(2 * R, HALF),
        spread_matrix(),
        (((0,), (0,)), ((), ())),
        preferred_element_type=jnp.float32,
    ).astype(out_ref.dtype)
    for a in range(4):
        s, u = divmod(a, 2)
        out_ref[:, pl.ds(a * R, R)] = ordered[u * WIDTH : (u + 1) * WIDTH, s * R : (s + 1) * R]


def high_kernel(taken_ref, feature_ref, table_ref, kept_ref, out_ref, local_ref, stacked_ref, semaphore):
    taken = taken_ref[...].reshape(2 * R, HALF)
    for hid in range(4):
        for u in range(2):
            local_ref[pl.ds(u * 128, 128), pl.ds(hid * WIDTH, WIDTH)] = taken[
                hid * 128 : (hid + 1) * 128, u * WIDTH : (u + 1) * WIDTH
            ]
    keep = pltpu.make_async_copy(local_ref, kept_ref, semaphore)
    keep.start()
    features = dot(local_ref[...], feature_ref[...])
    stacked_ref[pl.ds(0, R), pl.ds(0, HALF)] = features[:, :HALF].astype(jnp.bfloat16)
    stacked_ref[pl.ds(R, R), pl.ds(0, HALF)] = features[:, HALF:].astype(jnp.bfloat16)
    lane = lax.broadcasted_iota(jnp.int32, (R, 128), 1)
    first, middle = features[:, 0:1], features[:, HALF : HALF + 1]
    above = jnp.where(lane == 0, first, jnp.where(lane == 1, middle, 0.0))
    below = jnp.where(lane == 2, middle, 0.0)
    stacked_ref[pl.ds(0, R), pl.ds(HALF, 128)] = above.astype(jnp.bfloat16)
    stacked_ref[pl.ds(R, R), pl.ds(HALF, 128)] = below.astype(jnp.bfloat16)
    turned = dot(table_ref[...], stacked_ref[...])
    pair = lax.broadcasted_iota(jnp.int32, (2 * R, 128), 0)
    lane = lax.broadcasted_iota(jnp.int32, (2 * R, 128), 1)
    there = pair // 2
    alone = there < 2
    edge = turned[:, HALF:]
    single = jnp.where(jnp.logical_and(alone, pair % 2 == 1), edge[:, 2:3], edge[:, 0:1])
    single = jnp.where(jnp.logical_and(~alone, there % 2 == 1), edge[:, 1:2], single)
    head = jnp.where(lane == 0, single, turned[:, :128])
    sent = jnp.concatenate([head, turned[:, 128:HALF]], axis=1)
    out_ref[...] = sent.astype(out_ref.dtype).reshape(out_ref.shape)
    keep.wait()


def turn_kernel(table_ref, out_ref):
    residue = residue_of(lax.axis_index("hid") * SEQ_DEVICES + lax.axis_index("seq"))
    column = lax.broadcasted_iota(jnp.int32, (8, 2 * R), 1)
    opposite = jnp.where(residue == 0, 0, R - residue)
    row = lax.broadcasted_iota(jnp.int32, (8, 2 * R), 0)
    phase = jnp.where(row == 0, residue, opposite) * residue_of(column // 2)
    angle = phase.astype(jnp.float32) * (2.0 * math.pi / SEQ)
    sign = jnp.where(jnp.logical_or(row == 0, column % 2 == 0), 1.0, -1.0)
    cosine, sine = jnp.cos(angle) * sign, jnp.sin(angle) * sign
    for index in range(2):
        matrix = table_ref[0] * cosine[index : index + 1] + table_ref[1] * sine[index : index + 1]
        out_ref[index] = matrix.astype(out_ref.dtype)


def low_kernel(taken_ref, matrix_ref, own_ref, other_ref, wide_ref):
    scale = 1.0 / math.sqrt(SEQ * D)
    alone = jnp.logical_and(lax.axis_index("hid") == 0, lax.axis_index("seq") < 2)
    taken = taken_ref[...].reshape(2 * R, HALF)
    wide_ref[:, pl.ds(0, HALF)] = taken
    edge = taken[:, :128].astype(jnp.float32)
    row = lax.broadcasted_iota(jnp.int32, (2 * R, 128), 0)
    lane = lax.broadcasted_iota(jnp.int32, (2 * R, 128), 1)
    raised = pltpu.roll(pltpu.roll(edge, 2 * R - 1, 0), 1, 1)
    edge = jnp.where(row % 2 == 0, jnp.where(lane == 0, edge, raised), 0.0)
    wide_ref[:, pl.ds(HALF, 128)] = edge.astype(wide_ref.dtype)
    lane = lax.broadcasted_iota(jnp.int32, (R, 128), 1)
    single = jnp.logical_and(lane == 0, alone)
    for index, out_ref in enumerate((own_ref, other_ref)):
        usual = dot(matrix_ref[index], wide_ref[...]) * scale
        edge = usual[:, HALF + index : HALF + index + 1]
        out_ref[:, pl.ds(0, 128)] = jnp.where(single, edge, usual[:, :128]).astype(out_ref.dtype)
        out_ref[:, pl.ds(128, HALF - 128)] = usual[:, 128:HALF].astype(out_ref.dtype)


def whole_rows(parts):
    parts = parts.astype(jnp.float32)
    return parts[0:8] + parts[8:16] + parts[16:24]


def layer_kernel(
    own_any,
    received_any,
    mirror_any,
    local_any,
    inner_ref,
    outer_ref,
    payload_ref,
    ring_refs,
    swapped_refs,
    out_ref,
    own_ref,
    received_ref,
    mirror_ref,
    local_ref,
    around_ref,
    weights_ref,
    rows_ref,
    total_ref,
    folded_ref,
    semaphores,
):
    hid, seq = lax.axis_index("hid"), lax.axis_index("seq")
    core = lax.rem(seq, 2)
    crossed = jnp.logical_and(core == 1, jnp.logical_or(hid > 0, seq >= 2))

    def copy(source, target, index):
        return pltpu.make_async_copy(source, target, semaphores.at[index])

    inputs = [
        copy(received_any, received_ref, 0),
        copy(mirror_any, mirror_ref, 1),
        copy(own_any, own_ref, 2),
        copy(local_any, local_ref, 3),
    ]
    for each in inputs:
        each.start()
    inner_from = [(inner_ref, inner_ref)]
    outer_from = [(outer_ref, outer_ref)]
    small_from = [(payload_ref, payload_ref)]
    for i, j in ((0, 2), (2, 0), (1, 1)):
        pair = (ring_refs[i], swapped_refs[i])
        inner_from.append(tuple(each.at[pl.ds(0, D)] for each in pair))
        small_from.append(pair)
        outer_from.append(
            tuple(each.at[pl.ds(0, D)] for each in (swapped_refs[j], ring_refs[j]))
        )
    sources = [each for pair in zip(inner_from, outer_from) for each in pair]

    def small_copy(which, taken_by):
        source = small_from[which][taken_by].at[pl.ds(D, EXTRA)]
        return copy(source, around_ref.at[(0, 3, 1, 2)[which]], 4 + which)

    for taken_by in range(2):

        @pl.when(core == taken_by)
        def _():
            for which in range(4):
                small_copy(which, taken_by).start()
            for index, each in enumerate(sources):
                copy(each[taken_by], weights_ref.at[index], 8 + index).start()

    inputs += [small_copy(which, 0) for which in range(4)]
    for each in inputs:
        each.wait()
    for block in range(4):
        at = lax.rem(block - hid + 4, 4)
        sums = whole_rows(around_ref[at])
        for index in range(5):
            row, column = divmod(index, 4)
            rows_ref[index : index + 1, pl.ds(block * WIDTH, WIDTH)] = sums[
                row : row + 1, column * WIDTH : (column + 1) * WIDTH
            ]

    received = received_ref[...]
    own = own_ref[...]
    lane = lax.broadcasted_iota(jnp.int32, (R, HALF), 1)
    take = jnp.logical_and(lane == 0, crossed)
    low = jnp.where(take, received.astype(jnp.float32), own)
    high = jnp.where(take, own, dot(received, mirror_ref[...]))
    mixed = jnp.concatenate([low, high], axis=1)
    first_sum = local_ref[...].astype(jnp.float32) + mixed
    normed = norm_rows(first_sum, rows_ref[0:1, :], rows_ref[1:2, :]).astype(jnp.bfloat16)
    total_ref[...] = normed.astype(jnp.float32) + rows_ref[2:3, :]
    for index, distance in enumerate((0, 3, 1, 2)):
        for at in (2 * index, 2 * index + 1):
            copy(sources[at][0], weights_ref.at[at], 8 + at).wait()
        inner = dot(normed, weights_ref[2 * index]) + whole_rows(around_ref[distance])[2:3]
        active = jax.nn.gelu(inner, approximate=True).astype(jnp.bfloat16)
        total_ref[...] += dot(active, weights_ref[2 * index + 1])
    finished = norm_rows(total_ref[...], rows_ref[3:4, :], rows_ref[4:5, :]).astype(out_ref.dtype)
    for block in range(4):
        for u in range(2):
            folded_ref[pl.ds(block * 128, 128), pl.ds(u * WIDTH, WIDTH)] = finished[
                u * 128 : (u + 1) * 128, block * WIDTH : (block + 1) * WIDTH
            ]
    out_ref[...] = folded_ref[...].reshape(out_ref.shape)


VMEM = pl.BlockSpec(memory_space=pltpu.VMEM)
HBM = pl.BlockSpec(memory_space=pltpu.HBM)
ANYWHERE = pl.BlockSpec(memory_space=pl.ANY)
EXTRA = 32


def params(mebibytes):
    return pltpu.CompilerParams(vmem_limit_bytes=mebibytes * 2**20)


def array(shape, dtype=jnp.bfloat16):
    return jax.ShapeDtypeStruct(shape, dtype)


def pair_index(seq, hid):
    return seq * HID_DEVICES + hid % HID_DEVICES


def ring(value, sign):
    pairs = []
    for seq in range(SEQ_DEVICES):
        step = -sign if seq & 1 else sign
        for hid in range(HID_DEVICES):
            pairs.append((pair_index(seq, hid), pair_index(seq, hid + step)))
    return lax.ppermute(value, ("seq", "hid"), pairs)


def swap_cores(value):
    return lax.ppermute(value, "seq", [(seq, seq ^ 1) for seq in range(SEQ_DEVICES)])


def swap_mirrored(value):
    pairs = []
    for seq in range(SEQ_DEVICES):
        for hid in range(HID_DEVICES):
            alone = seq < 2 and hid == 0
            pairs.append((pair_index(seq, hid), pair_index(seq if alone else seq ^ 1, hid)))
    return lax.ppermute(value, ("seq", "hid"), pairs)


def shift_hid(value, step):
    pairs = [(hid, (hid + step) % HID_DEVICES) for hid in range(HID_DEVICES)]
    return lax.ppermute(value, "hid", pairs)


def low_matrices(after):
    table, _ = lax.optimization_barrier((jnp.asarray(LOW_TABLE), after))
    return pl.pallas_call(
        turn_kernel,
        out_shape=array((2, R, 2 * R)),
        in_specs=[VMEM],
        out_specs=VMEM,
        compiler_params=params(8),
        cost_estimate=pl.CostEstimate(flops=10**10, bytes_accessed=2 * 10**7, transcendentals=0),
    )(table)


def shards(
    tokens,
    first_gain,
    first_shift,
    inner_weight,
    inner_bias,
    outer_weight,
    outer_bias,
    second_gain,
    second_shift,
):
    bf16 = jnp.bfloat16
    f32 = jnp.float32

    payload = pl.pallas_call(
        payload_kernel,
        out_shape=array((D + EXTRA, D)),
        in_specs=[HBM] * 2 + [VMEM] * 6,
        out_specs=VMEM,
        scratch_shapes=[pltpu.VMEM((8, D), f32), pltpu.SemaphoreType.DMA],
        compiler_params=params(62),
    )(
        inner_weight,
        outer_weight,
        first_gain,
        first_shift,
        outer_bias,
        second_gain,
        second_shift,
        inner_bias,
    )
    ring_one = ring(payload, 1)

    tokens_t, _ = lax.optimization_barrier((tokens.T, payload))
    sent = pl.pallas_call(
        scatter_kernel,
        out_shape=array(CHUNKS),
        in_specs=[VMEM],
        out_specs=VMEM,
        scratch_shapes=[pltpu.VMEM((HALF, 2 * R), bf16)],
        compiler_params=params(8),
    )(tokens_t)
    taken = lax.all_to_all(sent, EVERY, 0, 0, tiled=True)

    matrices = low_matrices(sent)
    (ring_one, late), _ = lax.optimization_barrier(((ring_one, payload), matrices))
    ring_two, ring_three = ring(ring_one, 1), ring(late, -1)
    swap_one = swap_cores(ring_one)
    taken, _ = lax.optimization_barrier((taken, matrices))

    local, sent = pl.pallas_call(
        high_kernel,
        out_shape=(array((R, D)), array(CHUNKS)),
        in_specs=[VMEM] * 3,
        out_specs=(HBM, VMEM),
        scratch_shapes=[
            pltpu.VMEM((R, D), bf16),
            pltpu.VMEM((2 * R, 2 * R), bf16),
            pltpu.SemaphoreType.DMA,
        ],
        compiler_params=params(16),
    )(taken, jnp.asarray(FEATURE), jnp.asarray(HIGH_TABLE))
    taken = lax.all_to_all(sent, EVERY, 0, 0, tiled=True)

    (ring_two, ring_three), _ = lax.optimization_barrier(((ring_two, ring_three), taken))
    swap_two, swap_three = swap_cores(ring_two), swap_cores(ring_three)

    own, other = pl.pallas_call(
        low_kernel,
        out_shape=(array((R, HALF), f32), array((R, HALF))),
        in_specs=[VMEM] * 2,
        out_specs=(VMEM, VMEM),
        scratch_shapes=[pltpu.VMEM((2 * R, 2 * R), bf16)],
        compiler_params=params(8),
    )(taken, matrices)
    received = swap_mirrored(other)

    def layer(*refs):
        return layer_kernel(*refs[:7], refs[7:10], refs[10:13], *refs[13:])

    sent = pl.pallas_call(
        layer,
        out_shape=array(CHUNKS),
        in_specs=[ANYWHERE] * 2 + [HBM] * 2 + [ANYWHERE] * 9,
        out_specs=VMEM,
        scratch_shapes=[
            pltpu.VMEM((R, HALF), f32),
            pltpu.VMEM((R, HALF), bf16),
            pltpu.VMEM((HALF, HALF), bf16),
            pltpu.VMEM((R, D), bf16),
            pltpu.VMEM((4, EXTRA, D), bf16),
            pltpu.VMEM((8, D, D), bf16),
            pltpu.VMEM((8, D), f32),
            pltpu.VMEM((R, D), f32),
            pltpu.VMEM((2 * R, HALF), bf16),
            pltpu.SemaphoreType.DMA((16,)),
        ],
        compiler_params=params(52),
    )(
        own,
        received,
        jnp.asarray(MIRROR),
        local,
        inner_weight,
        outer_weight,
        payload,
        ring_one,
        ring_two,
        ring_three,
        swap_one,
        swap_two,
        swap_three,
    )
    taken = lax.all_to_all(sent, EVERY, 0, 0, tiled=True)

    return pl.pallas_call(
        gather_kernel,
        out_shape=array(tokens.shape[::-1]),
        in_specs=[VMEM],
        out_specs=VMEM,
        compiler_params=params(8),
    )(taken).T


def solution(mesh):
    return jax.shard_map(
        shards,
        mesh=mesh,
        in_specs=(
            P("seq", "hid"),
            P("hid"),
            P("hid"),
            P(None, "hid"),
            P("hid"),
            P("hid", None),
            P("hid"),
            P("hid"),
            P("hid"),
        ),
        out_specs=P("seq", "hid"),
        check_vma=False,
    )
```

```python
import functools
import math

import jax
import jax.numpy as jnp
import ml_dtypes
import numpy as np
from jax import lax
from jax.experimental import pallas as pl
from jax.experimental.pallas import tpu as pltpu
from jax.sharding import PartitionSpec as P

D = 768
HALF = D // 2
SEQ = 65536
R = 256
SEQ_DEVICES = 64
HID_DEVICES = 4
WIDTH = D // HID_DEVICES
EVERY = ("hid", "seq")
CHUNKS = (R, 2, HALF)
BF16 = ml_dtypes.bfloat16


def residues():
    place = np.arange(R)
    hid, seq = place // SEQ_DEVICES, place % SEQ_DEVICES
    chip = (seq >> 1) * HID_DEVICES + hid
    core = seq & 1
    return np.where(core == 0, chip, np.where(chip == 0, R // 2, R - chip)), chip, core


RESIDUE, CHIP, CORE = residues()
ROW = np.arange(R)
HIGH = 4 * (ROW % 128 // 2) + 2 * (ROW % 2) + ROW // 128


def cosine_sine(phase, period):
    angle = 2.0 * np.pi * (phase % period).astype(np.float64) / period
    return np.cos(angle), np.sin(angle)


def feature_table():
    rows = np.arange(D, dtype=np.int64)[:, None]
    columns = np.arange(HALF + 1, dtype=np.int64)[None, :]
    angle = np.float32(2.0 * math.pi / D) * (rows * columns % D).astype(np.float32)
    cosine = np.cos(angle.astype(np.float64)).astype(BF16)
    sine = (-np.sin(angle.astype(np.float64))).astype(BF16)
    sine[:, 0] = cosine[:, HALF]
    return np.concatenate([cosine[:, :HALF], sine[:, :HALF]], axis=1)


def pairs_of_rows(even, odd):
    return np.stack([even, odd], axis=1).reshape(2 * even.shape[0], -1)


def high_table():
    cosine, sine = cosine_sine(RESIDUE[:, None] * HIGH[None, :], R)
    even = np.concatenate([cosine, sine], axis=1)
    odd = np.concatenate([-sine, cosine], axis=1)
    return pairs_of_rows(even, odd).astype(BF16)


def low_table():
    cosine, sine = cosine_sine(HIGH[:, None] * RESIDUE[None, :], R)
    table = np.stack([pairs_of_rows(cosine.T, sine.T).T, pairs_of_rows(-sine.T, cosine.T).T])
    return table.astype(np.float32)


FEATURE = feature_table()
HIGH_TABLE = high_table()
LOW_TABLE = low_table()
LANE = np.arange(HALF)
MIRROR = (LANE[:, None] == (HALF - LANE[None, :]) % HALF).astype(BF16)


def dot(left, right):
    return jnp.dot(left, right, preferred_element_type=jnp.float32)


def norm_rows(values, gain, shift):
    mean = jnp.mean(values, axis=1, keepdims=True)
    spread = jnp.mean(values * values, axis=1, keepdims=True) - mean * mean
    return (values - mean) * lax.rsqrt(spread + 1e-05) * gain + shift


def residue_of(place):
    hid, seq = place // SEQ_DEVICES, place % SEQ_DEVICES
    chip = seq // 2 * HID_DEVICES + hid
    late = jnp.where(chip == 0, R // 2, R - chip)
    return jnp.where(seq % 2 == 0, chip, late)


def spread_matrix():
    pair = lax.broadcasted_iota(jnp.int32, (2 * R, 1), 0)
    target = pair % 2 * R + residue_of(pair // 2)
    column = lax.broadcasted_iota(jnp.int32, (1, 2 * R), 1)
    return jnp.where(target == column, 1.0, 0.0).astype(jnp.bfloat16)


def payload_kernel(inner_ref, outer_ref, *rest):
    *vector_refs, payload_ref, rows_ref, semaphore = rest
    core = lax.rem(lax.axis_index("seq"), 2)
    weights = payload_ref.at[pl.ds(0, D)]

    @pl.when(core == 0)
    def _():
        pltpu.make_async_copy(inner_ref, weights, semaphore).start()

    @pl.when(core == 1)
    def _():
        pltpu.make_async_copy(outer_ref, weights, semaphore).start()

    rows_ref[...] = jnp.zeros_like(rows_ref)
    for index, each in enumerate(vector_refs):
        row, at = divmod(index, 4) if index < 5 else (2, 0)
        rows_ref[row : row + 1, pl.ds(at * WIDTH, each.shape[0])] = each[...][None, :]
    rest = rows_ref[...]
    pieces = []
    for _ in range(3):
        pieces.append(rest.astype(jnp.bfloat16).astype(jnp.float32))
        rest = rest - pieces[-1]
    pieces.append(jnp.zeros_like(rest))
    payload_ref[pl.ds(D, EXTRA), :] = jnp.concatenate(pieces, axis=0).astype(jnp.bfloat16)
    pltpu.make_async_copy(inner_ref, weights, semaphore).wait()


def scatter_kernel(tokens_ref, out_ref, wide_ref):
    for a in range(4):
        s, u = divmod(a, 2)
        wide_ref[pl.ds(u * WIDTH, WIDTH), pl.ds(s * R, R)] = tokens_ref[:, pl.ds(a * R, R)]
    spread = lax.dot_general(
        spread_matrix(),
        wide_ref[...],
        (((1,), (1,)), ((), ())),
        preferred_element_type=jnp.float32,
    )
    out_ref[...] = spread.astype(out_ref.dtype).reshape(out_ref.shape)


def gather_kernel(taken_ref, out_ref):
    ordered = lax.dot_general(
        taken_ref[...].reshape(2 * R, HALF),
        spread_matrix(),
        (((0,), (0,)), ((), ())),
        preferred_element_type=jnp.float32,
    ).astype(out_ref.dtype)
    for a in range(4):
        s, u = divmod(a, 2)
        out_ref[:, pl.ds(a * R, R)] = ordered[u * WIDTH : (u + 1) * WIDTH, s * R : (s + 1) * R]


def high_kernel(taken_ref, feature_ref, table_ref, kept_ref, out_ref, local_ref, stacked_ref, semaphore):
    taken = taken_ref[...].reshape(2 * R, HALF)
    for hid in range(4):
        for u in range(2):
            local_ref[pl.ds(u * 128, 128), pl.ds(hid * WIDTH, WIDTH)] = taken[
                hid * 128 : (hid + 1) * 128, u * WIDTH : (u + 1) * WIDTH
            ]
    keep = pltpu.make_async_copy(local_ref, kept_ref, semaphore)
    keep.start()
    features = dot(local_ref[...], feature_ref[...])
    stacked_ref[pl.ds(0, R), pl.ds(0, HALF)] = features[:, :HALF].astype(jnp.bfloat16)
    stacked_ref[pl.ds(R, R), pl.ds(0, HALF)] = features[:, HALF:].astype(jnp.bfloat16)
    lane = lax.broadcasted_iota(jnp.int32, (R, 128), 1)
    first, middle = features[:, 0:1], features[:, HALF : HALF + 1]
    above = jnp.where(lane == 0, first, jnp.where(lane == 1, middle, 0.0))
    below = jnp.where(lane == 2, middle, 0.0)
    stacked_ref[pl.ds(0, R), pl.ds(HALF, 128)] = above.astype(jnp.bfloat16)
    stacked_ref[pl.ds(R, R), pl.ds(HALF, 128)] = below.astype(jnp.bfloat16)
    turned = dot(table_ref[...], stacked_ref[...])
    pair = lax.broadcasted_iota(jnp.int32, (2 * R, 128), 0)
    lane = lax.broadcasted_iota(jnp.int32, (2 * R, 128), 1)
    there = pair // 2
    alone = there < 2
    edge = turned[:, HALF:]
    single = jnp.where(jnp.logical_and(alone, pair % 2 == 1), edge[:, 2:3], edge[:, 0:1])
    single = jnp.where(jnp.logical_and(~alone, there % 2 == 1), edge[:, 1:2], single)
    head = jnp.where(lane == 0, single, turned[:, :128])
    sent = jnp.concatenate([head, turned[:, 128:HALF]], axis=1)
    out_ref[...] = sent.astype(out_ref.dtype).reshape(out_ref.shape)
    keep.wait()


def turn_kernel(opposed, table_ref, out_ref):
    residue = residue_of(lax.axis_index("hid") * SEQ_DEVICES + lax.axis_index("seq"))
    column = lax.broadcasted_iota(jnp.int32, (8, 2 * R), 1)
    opposite = jnp.where(residue == 0, 0, R - residue)
    row = lax.broadcasted_iota(jnp.int32, (8, 2 * R), 0)
    phase = jnp.where(row == 0, residue, opposite) * residue_of(column // 2)
    angle = phase.astype(jnp.float32) * (2.0 * math.pi / SEQ)
    sign = jnp.where(jnp.logical_or(row == 0, column % 2 == 0), 1.0, -1.0)
    cosine, sine = jnp.cos(angle) * sign, jnp.sin(angle) * sign
    index = int(opposed)
    matrix = table_ref[0] * cosine[index : index + 1] + table_ref[1] * sine[index : index + 1]
    out_ref[...] = matrix.astype(out_ref.dtype)


def low_kernel(taken_ref, first_ref, second_ref, own_ref, other_ref, wide_ref):
    scale = 1.0 / math.sqrt(SEQ * D)
    alone = jnp.logical_and(lax.axis_index("hid") == 0, lax.axis_index("seq") < 2)
    taken = taken_ref[...].reshape(2 * R, HALF)
    wide_ref[:, pl.ds(0, HALF)] = taken
    edge = taken[:, :128].astype(jnp.float32)
    row = lax.broadcasted_iota(jnp.int32, (2 * R, 128), 0)
    lane = lax.broadcasted_iota(jnp.int32, (2 * R, 128), 1)
    raised = pltpu.roll(pltpu.roll(edge, 2 * R - 1, 0), 1, 1)
    edge = jnp.where(row % 2 == 0, jnp.where(lane == 0, edge, raised), 0.0)
    wide_ref[:, pl.ds(HALF, 128)] = edge.astype(wide_ref.dtype)
    lane = lax.broadcasted_iota(jnp.int32, (R, 128), 1)
    single = jnp.logical_and(lane == 0, alone)
    for index, (matrix_ref, out_ref) in enumerate(((first_ref, own_ref), (second_ref, other_ref))):
        usual = dot(matrix_ref[...], wide_ref[...]) * scale
        edge = usual[:, HALF + index : HALF + index + 1]
        out_ref[:, pl.ds(0, 128)] = jnp.where(single, edge, usual[:, :128]).astype(out_ref.dtype)
        out_ref[:, pl.ds(128, HALF - 128)] = usual[:, 128:HALF].astype(out_ref.dtype)


def whole_rows(parts):
    parts = parts.astype(jnp.float32)
    return parts[0:8] + parts[8:16] + parts[16:24]


def layer_kernel(
    own_any,
    received_any,
    mirror_any,
    local_any,
    inner_ref,
    outer_ref,
    payload_ref,
    ring_refs,
    swapped_refs,
    out_ref,
    own_ref,
    received_ref,
    mirror_ref,
    local_ref,
    around_ref,
    weights_ref,
    rows_ref,
    total_ref,
    folded_ref,
    semaphores,
):
    hid, seq = lax.axis_index("hid"), lax.axis_index("seq")
    core = lax.rem(seq, 2)
    crossed = jnp.logical_and(core == 1, jnp.logical_or(hid > 0, seq >= 2))

    def copy(source, target, index):
        return pltpu.make_async_copy(source, target, semaphores.at[index])

    inputs = [
        copy(received_any, received_ref, 0),
        copy(mirror_any, mirror_ref, 1),
        copy(own_any, own_ref, 2),
        copy(local_any, local_ref, 3),
    ]
    for each in inputs:
        each.start()
    inner_from = [(inner_ref, inner_ref)]
    outer_from = [(outer_ref, outer_ref)]
    small_from = [(payload_ref, payload_ref)]
    for i, j in ((0, 2), (2, 0), (1, 1)):
        pair = (ring_refs[i], swapped_refs[i])
        inner_from.append(tuple(each.at[pl.ds(0, D)] for each in pair))
        small_from.append(pair)
        outer_from.append(
            tuple(each.at[pl.ds(0, D)] for each in (swapped_refs[j], ring_refs[j]))
        )
    sources = [each for pair in zip(inner_from, outer_from) for each in pair]

    def small_copy(which, taken_by):
        source = small_from[which][taken_by].at[pl.ds(D, EXTRA)]
        return copy(source, around_ref.at[(0, 3, 1, 2)[which]], 4 + which)

    for taken_by in range(2):

        @pl.when(core == taken_by)
        def _():
            for which in range(4):
                small_copy(which, taken_by).start()
            for index, each in enumerate(sources):
                copy(each[taken_by], weights_ref.at[index], 8 + index).start()

    inputs += [small_copy(which, 0) for which in range(4)]
    for each in inputs:
        each.wait()
    for block in range(4):
        at = lax.rem(block - hid + 4, 4)
        sums = whole_rows(around_ref[at])
        for index in range(5):
            row, column = divmod(index, 4)
            rows_ref[index : index + 1, pl.ds(block * WIDTH, WIDTH)] = sums[
                row : row + 1, column * WIDTH : (column + 1) * WIDTH
            ]

    received = received_ref[...]
    own = own_ref[...]
    lane = lax.broadcasted_iota(jnp.int32, (R, HALF), 1)
    take = jnp.logical_and(lane == 0, crossed)
    low = jnp.where(take, received.astype(jnp.float32), own)
    high = jnp.where(take, own, dot(received, mirror_ref[...]))
    mixed = jnp.concatenate([low, high], axis=1)
    first_sum = local_ref[...].astype(jnp.float32) + mixed
    normed = norm_rows(first_sum, rows_ref[0:1, :], rows_ref[1:2, :]).astype(jnp.bfloat16)
    total_ref[...] = normed.astype(jnp.float32) + rows_ref[2:3, :]
    def project(index):
        for at in (2 * index, 2 * index + 1):
            copy(sources[at][0], weights_ref.at[at], 8 + at).wait()
        return dot(normed, weights_ref[2 * index])

    later = project(0)
    for index, distance in enumerate((0, 3, 1, 2)):
        inner = later + whole_rows(around_ref[distance])[2:3]
        if index < 3:
            later = project(index + 1)
        active = jax.nn.gelu(inner, approximate=True).astype(jnp.bfloat16)
        total_ref[...] += dot(active, weights_ref[2 * index + 1])
    finished = norm_rows(total_ref[...], rows_ref[3:4, :], rows_ref[4:5, :]).astype(out_ref.dtype)
    for block in range(4):
        for u in range(2):
            folded_ref[pl.ds(block * 128, 128), pl.ds(u * WIDTH, WIDTH)] = finished[
                u * 128 : (u + 1) * 128, block * WIDTH : (block + 1) * WIDTH
            ]
    out_ref[...] = folded_ref[...].reshape(out_ref.shape)


VMEM = pl.BlockSpec(memory_space=pltpu.VMEM)
HBM = pl.BlockSpec(memory_space=pltpu.HBM)
ANYWHERE = pl.BlockSpec(memory_space=pl.ANY)
EXTRA = 32
HIDDEN = pl.CostEstimate(flops=10**10, bytes_accessed=2 * 10**7, transcendentals=0)


def params(mebibytes):
    return pltpu.CompilerParams(vmem_limit_bytes=mebibytes * 2**20)


def array(shape, dtype=jnp.bfloat16):
    return jax.ShapeDtypeStruct(shape, dtype)


def pair_index(seq, hid):
    return seq * HID_DEVICES + hid % HID_DEVICES


def ring(value, sign):
    pairs = []
    for seq in range(SEQ_DEVICES):
        step = -sign if seq & 1 else sign
        for hid in range(HID_DEVICES):
            pairs.append((pair_index(seq, hid), pair_index(seq, hid + step)))
    return lax.ppermute(value, ("seq", "hid"), pairs)


def swap_cores(value):
    return lax.ppermute(value, "seq", [(seq, seq ^ 1) for seq in range(SEQ_DEVICES)])


def swap_mirrored(value):
    pairs = []
    for seq in range(SEQ_DEVICES):
        for hid in range(HID_DEVICES):
            alone = seq < 2 and hid == 0
            pairs.append((pair_index(seq, hid), pair_index(seq if alone else seq ^ 1, hid)))
    return lax.ppermute(value, ("seq", "hid"), pairs)


def shift_hid(value, step):
    pairs = [(hid, (hid + step) % HID_DEVICES) for hid in range(HID_DEVICES)]
    return lax.ppermute(value, "hid", pairs)


def low_matrix(opposed, after):
    table, _ = lax.optimization_barrier((jnp.asarray(LOW_TABLE), after))
    return pl.pallas_call(
        functools.partial(turn_kernel, opposed),
        out_shape=array((R, 2 * R)),
        in_specs=[VMEM],
        out_specs=VMEM,
        compiler_params=params(8),
        cost_estimate=HIDDEN,
    )(table)


def shards(
    tokens,
    first_gain,
    first_shift,
    inner_weight,
    inner_bias,
    outer_weight,
    outer_bias,
    second_gain,
    second_shift,
):
    bf16 = jnp.bfloat16
    f32 = jnp.float32

    payload = pl.pallas_call(
        payload_kernel,
        out_shape=array((D + EXTRA, D)),
        in_specs=[HBM] * 2 + [VMEM] * 6,
        out_specs=VMEM,
        scratch_shapes=[pltpu.VMEM((8, D), f32), pltpu.SemaphoreType.DMA],
        compiler_params=params(62),
    )(
        inner_weight,
        outer_weight,
        first_gain,
        first_shift,
        outer_bias,
        second_gain,
        second_shift,
        inner_bias,
    )
    ring_one = ring(payload, 1)

    tokens_t, _ = lax.optimization_barrier((tokens.T, payload))
    sent = pl.pallas_call(
        scatter_kernel,
        out_shape=array(CHUNKS),
        in_specs=[VMEM],
        out_specs=VMEM,
        scratch_shapes=[pltpu.VMEM((HALF, 2 * R), bf16)],
        compiler_params=params(8),
    )(tokens_t)
    taken = lax.all_to_all(sent, EVERY, 0, 0, tiled=True)

    own_matrix = low_matrix(False, sent)
    (ring_one, late), _ = lax.optimization_barrier(((ring_one, payload), own_matrix))
    ring_two, ring_three = ring(ring_one, 1), ring(late, -1)
    swap_one = swap_cores(ring_one)
    taken, _ = lax.optimization_barrier((taken, own_matrix))

    local, sent = pl.pallas_call(
        high_kernel,
        out_shape=(array((R, D)), array(CHUNKS)),
        in_specs=[VMEM] * 3,
        out_specs=(HBM, VMEM),
        scratch_shapes=[
            pltpu.VMEM((R, D), bf16),
            pltpu.VMEM((2 * R, 2 * R), bf16),
            pltpu.SemaphoreType.DMA,
        ],
        compiler_params=params(16),
    )(taken, jnp.asarray(FEATURE), jnp.asarray(HIGH_TABLE))
    taken = lax.all_to_all(sent, EVERY, 0, 0, tiled=True)

    other_matrix = low_matrix(True, sent)
    (ring_two, ring_three), _ = lax.optimization_barrier(((ring_two, ring_three), other_matrix))
    swap_two, swap_three = swap_cores(ring_two), swap_cores(ring_three)

    own, other = pl.pallas_call(
        low_kernel,
        out_shape=(array((R, HALF), f32), array((R, HALF))),
        in_specs=[VMEM] * 3,
        out_specs=(VMEM, VMEM),
        scratch_shapes=[pltpu.VMEM((2 * R, 2 * R), bf16)],
        compiler_params=params(8),
        cost_estimate=HIDDEN,
    )(taken, own_matrix, other_matrix)
    received = swap_mirrored(other)

    def layer(*refs):
        return layer_kernel(*refs[:7], refs[7:10], refs[10:13], *refs[13:])

    sent = pl.pallas_call(
        layer,
        out_shape=array(CHUNKS),
        in_specs=[ANYWHERE] * 2 + [HBM] * 2 + [ANYWHERE] * 9,
        out_specs=VMEM,
        scratch_shapes=[
            pltpu.VMEM((R, HALF), f32),
            pltpu.VMEM((R, HALF), bf16),
            pltpu.VMEM((HALF, HALF), bf16),
            pltpu.VMEM((R, D), bf16),
            pltpu.VMEM((4, EXTRA, D), bf16),
            pltpu.VMEM((8, D, D), bf16),
            pltpu.VMEM((8, D), f32),
            pltpu.VMEM((R, D), f32),
            pltpu.VMEM((2 * R, HALF), bf16),
            pltpu.SemaphoreType.DMA((16,)),
        ],
        compiler_params=params(52),
    )(
        own,
        received,
        jnp.asarray(MIRROR),
        local,
        inner_weight,
        outer_weight,
        payload,
        ring_one,
        ring_two,
        ring_three,
        swap_one,
        swap_two,
        swap_three,
    )
    taken = lax.all_to_all(sent, EVERY, 0, 0, tiled=True)

    return pl.pallas_call(
        gather_kernel,
        out_shape=array(tokens.shape[::-1]),
        in_specs=[VMEM],
        out_specs=VMEM,
        compiler_params=params(8),
    )(taken).T


def solution(mesh):
    return jax.shard_map(
        shards,
        mesh=mesh,
        in_specs=(
            P("seq", "hid"),
            P("hid"),
            P("hid"),
            P(None, "hid"),
            P("hid"),
            P("hid", None),
            P("hid"),
            P("hid"),
            P("hid"),
        ),
        out_specs=P("seq", "hid"),
        check_vma=False,
    )
```

```python
import functools
import math

import jax
import jax.numpy as jnp
import ml_dtypes
import numpy as np
from jax import lax
from jax.experimental import pallas as pl
from jax.experimental.pallas import tpu as pltpu
from jax.sharding import PartitionSpec as P

D = 768
HALF = D // 2
SEQ = 65536
R = 256
SEQ_DEVICES = 64
HID_DEVICES = 4
WIDTH = D // HID_DEVICES
EVERY = ("hid", "seq")
CHUNKS = (R, 2, HALF)
BF16 = ml_dtypes.bfloat16


def residues():
    place = np.arange(R)
    hid, seq = place // SEQ_DEVICES, place % SEQ_DEVICES
    chip = (seq >> 1) * HID_DEVICES + hid
    core = seq & 1
    return np.where(core == 0, chip, np.where(chip == 0, R // 2, R - chip)), chip, core


RESIDUE, CHIP, CORE = residues()
ROW = np.arange(R)
HIGH = 4 * (ROW % 128 // 2) + 2 * (ROW % 2) + ROW // 128


def cosine_sine(phase, period):
    angle = 2.0 * np.pi * (phase % period).astype(np.float64) / period
    return np.cos(angle), np.sin(angle)


def feature_table():
    rows = np.arange(D, dtype=np.int64)[:, None]
    columns = np.arange(HALF + 1, dtype=np.int64)[None, :]
    angle = np.float32(2.0 * math.pi / D) * (rows * columns % D).astype(np.float32)
    cosine = np.cos(angle.astype(np.float64)).astype(BF16)
    sine = (-np.sin(angle.astype(np.float64))).astype(BF16)
    sine[:, 0] = cosine[:, HALF]
    return np.concatenate([cosine[:, :HALF], sine[:, :HALF]], axis=1)


def pairs_of_rows(even, odd):
    return np.stack([even, odd], axis=1).reshape(2 * even.shape[0], -1)


def high_table():
    cosine, sine = cosine_sine(RESIDUE[:, None] * HIGH[None, :], R)
    even = np.concatenate([cosine, sine], axis=1)
    odd = np.concatenate([-sine, cosine], axis=1)
    return pairs_of_rows(even, odd).astype(BF16)


def low_table():
    cosine, sine = cosine_sine(HIGH[:, None] * RESIDUE[None, :], R)
    table = np.stack([pairs_of_rows(cosine.T, sine.T).T, pairs_of_rows(-sine.T, cosine.T).T])
    return table.astype(np.float32)


FEATURE = feature_table()
HIGH_TABLE = high_table()
LOW_TABLE = low_table()
LANE = np.arange(HALF)
MIRROR = (LANE[:, None] == (HALF - LANE[None, :]) % HALF).astype(BF16)


def dot(left, right):
    return jnp.dot(left, right, preferred_element_type=jnp.float32)


def norm_rows(values, gain, shift):
    mean = jnp.mean(values, axis=1, keepdims=True)
    spread = jnp.mean(values * values, axis=1, keepdims=True) - mean * mean
    return (values - mean) * lax.rsqrt(spread + 1e-05) * gain + shift


def residue_of(place):
    hid, seq = place // SEQ_DEVICES, place % SEQ_DEVICES
    chip = seq // 2 * HID_DEVICES + hid
    late = jnp.where(chip == 0, R // 2, R - chip)
    return jnp.where(seq % 2 == 0, chip, late)


def spread_matrix():
    pair = lax.broadcasted_iota(jnp.int32, (2 * R, 1), 0)
    target = pair % 2 * R + residue_of(pair // 2)
    column = lax.broadcasted_iota(jnp.int32, (1, 2 * R), 1)
    return jnp.where(target == column, 1.0, 0.0).astype(jnp.bfloat16)


def payload_kernel(inner_ref, outer_ref, *rest):
    sources, rest = rest[:6], rest[6:]
    payload_ref, held_ref, parts_ref, rows_ref, *vector_refs, semaphores = rest
    vectors = [
        pltpu.make_async_copy(source, target, semaphores.at[9 + at])
        for at, (source, target) in enumerate(zip(sources, vector_refs))
    ]
    for each in vectors:
        each.start()
    core = lax.rem(lax.axis_index("seq"), 2)
    pieces_of_rows = [pl.ds(at * WIDTH, WIDTH) for at in range(4)]

    def fetch(source, at):
        rows = pieces_of_rows[at]
        return pltpu.make_async_copy(source.at[rows], held_ref.at[rows], semaphores.at[at])

    @pl.when(core == 0)
    def _():
        for at in range(4):
            fetch(inner_ref, at).start()

    @pl.when(core == 1)
    def _():
        for at in range(4):
            fetch(outer_ref, at).start()

    for each in vectors:
        each.wait()
    rows_ref[...] = jnp.zeros_like(rows_ref)
    for index, each in enumerate(vector_refs):
        row, at = divmod(index, 4) if index < 5 else (2, 0)
        rows_ref[row : row + 1, pl.ds(at * WIDTH, each.shape[0])] = each[...][None, :]
    rest = rows_ref[...]
    pieces = []
    for _ in range(3):
        pieces.append(rest.astype(jnp.bfloat16).astype(jnp.float32))
        rest = rest - pieces[-1]
    pieces.append(jnp.zeros_like(rest))
    parts_ref[...] = jnp.concatenate(pieces, axis=0).astype(jnp.bfloat16)
    copies = [pltpu.make_async_copy(parts_ref, payload_ref.at[pl.ds(D, EXTRA)], semaphores.at[8])]
    copies[0].start()
    for at, rows in enumerate(pieces_of_rows):
        fetch(inner_ref, at).wait()
        copies.append(
            pltpu.make_async_copy(held_ref.at[rows], payload_ref.at[rows], semaphores.at[4 + at])
        )
        copies[-1].start()
    for each in copies:
        each.wait()


def scatter_kernel(tokens_ref, out_ref, wide_ref):
    for a in range(4):
        s, u = divmod(a, 2)
        wide_ref[pl.ds(u * WIDTH, WIDTH), pl.ds(s * R, R)] = tokens_ref[:, pl.ds(a * R, R)]
    spread = lax.dot_general(
        spread_matrix(),
        wide_ref[...],
        (((1,), (1,)), ((), ())),
        preferred_element_type=jnp.float32,
    )
    out_ref[...] = spread.astype(out_ref.dtype).reshape(out_ref.shape)


def gather_kernel(taken_ref, out_ref):
    ordered = lax.dot_general(
        taken_ref[...].reshape(2 * R, HALF),
        spread_matrix(),
        (((0,), (0,)), ((), ())),
        preferred_element_type=jnp.float32,
    ).astype(out_ref.dtype)
    for a in range(4):
        s, u = divmod(a, 2)
        out_ref[:, pl.ds(a * R, R)] = ordered[u * WIDTH : (u + 1) * WIDTH, s * R : (s + 1) * R]


def high_kernel(taken_ref, feature_ref, table_ref, kept_ref, out_ref, local_ref, stacked_ref, semaphore):
    taken = taken_ref[...].reshape(2 * R, HALF)
    for hid in range(4):
        for u in range(2):
            local_ref[pl.ds(u * 128, 128), pl.ds(hid * WIDTH, WIDTH)] = taken[
                hid * 128 : (hid + 1) * 128, u * WIDTH : (u + 1) * WIDTH
            ]
    keep = pltpu.make_async_copy(local_ref, kept_ref, semaphore)
    keep.start()
    features = dot(local_ref[...], feature_ref[...])
    stacked_ref[pl.ds(0, R), pl.ds(0, HALF)] = features[:, :HALF].astype(jnp.bfloat16)
    stacked_ref[pl.ds(R, R), pl.ds(0, HALF)] = features[:, HALF:].astype(jnp.bfloat16)
    lane = lax.broadcasted_iota(jnp.int32, (R, 128), 1)
    first, middle = features[:, 0:1], features[:, HALF : HALF + 1]
    above = jnp.where(lane == 0, first, jnp.where(lane == 1, middle, 0.0))
    below = jnp.where(lane == 2, middle, 0.0)
    stacked_ref[pl.ds(0, R), pl.ds(HALF, 128)] = above.astype(jnp.bfloat16)
    stacked_ref[pl.ds(R, R), pl.ds(HALF, 128)] = below.astype(jnp.bfloat16)
    turned = dot(table_ref[...], stacked_ref[...])
    pair = lax.broadcasted_iota(jnp.int32, (2 * R, 128), 0)
    lane = lax.broadcasted_iota(jnp.int32, (2 * R, 128), 1)
    there = pair // 2
    alone = there < 2
    edge = turned[:, HALF:]
    single = jnp.where(jnp.logical_and(alone, pair % 2 == 1), edge[:, 2:3], edge[:, 0:1])
    single = jnp.where(jnp.logical_and(~alone, there % 2 == 1), edge[:, 1:2], single)
    head = jnp.where(lane == 0, single, turned[:, :128])
    sent = jnp.concatenate([head, turned[:, 128:HALF]], axis=1)
    out_ref[...] = sent.astype(out_ref.dtype).reshape(out_ref.shape)
    keep.wait()


def turn_kernel(opposed, table_ref, out_ref):
    residue = residue_of(lax.axis_index("hid") * SEQ_DEVICES + lax.axis_index("seq"))
    column = lax.broadcasted_iota(jnp.int32, (8, 2 * R), 1)
    opposite = jnp.where(residue == 0, 0, R - residue)
    row = lax.broadcasted_iota(jnp.int32, (8, 2 * R), 0)
    phase = jnp.where(row == 0, residue, opposite) * residue_of(column // 2)
    angle = phase.astype(jnp.float32) * (2.0 * math.pi / SEQ)
    sign = jnp.where(jnp.logical_or(row == 0, column % 2 == 0), 1.0, -1.0)
    cosine, sine = jnp.cos(angle) * sign, jnp.sin(angle) * sign
    index = int(opposed)
    matrix = table_ref[0] * cosine[index : index + 1] + table_ref[1] * sine[index : index + 1]
    out_ref[...] = matrix.astype(out_ref.dtype)


def low_kernel(taken_ref, first_ref, second_ref, own_ref, other_ref, wide_ref):
    scale = 1.0 / math.sqrt(SEQ * D)
    alone = jnp.logical_and(lax.axis_index("hid") == 0, lax.axis_index("seq") < 2)
    taken = taken_ref[...].reshape(2 * R, HALF)
    wide_ref[:, pl.ds(0, HALF)] = taken
    edge = taken[:, :128].astype(jnp.float32)
    row = lax.broadcasted_iota(jnp.int32, (2 * R, 128), 0)
    lane = lax.broadcasted_iota(jnp.int32, (2 * R, 128), 1)
    raised = pltpu.roll(pltpu.roll(edge, 2 * R - 1, 0), 1, 1)
    edge = jnp.where(row % 2 == 0, jnp.where(lane == 0, edge, raised), 0.0)
    wide_ref[:, pl.ds(HALF, 128)] = edge.astype(wide_ref.dtype)
    lane = lax.broadcasted_iota(jnp.int32, (R, 128), 1)
    single = jnp.logical_and(lane == 0, alone)
    for index, (matrix_ref, out_ref) in enumerate(((first_ref, own_ref), (second_ref, other_ref))):
        usual = dot(matrix_ref[...], wide_ref[...]) * scale
        edge = usual[:, HALF + index : HALF + index + 1]
        out_ref[:, pl.ds(0, 128)] = jnp.where(single, edge, usual[:, :128]).astype(out_ref.dtype)
        out_ref[:, pl.ds(128, HALF - 128)] = usual[:, 128:HALF].astype(out_ref.dtype)


def whole_rows(parts):
    parts = parts.astype(jnp.float32)
    return parts[0:8] + parts[8:16] + parts[16:24]


def layer_kernel(
    own_any,
    received_any,
    mirror_any,
    local_any,
    inner_ref,
    outer_ref,
    payload_ref,
    ring_refs,
    swapped_refs,
    out_ref,
    own_ref,
    received_ref,
    mirror_ref,
    local_ref,
    around_ref,
    weights_ref,
    rows_ref,
    total_ref,
    folded_ref,
    semaphores,
):
    hid, seq = lax.axis_index("hid"), lax.axis_index("seq")
    core = lax.rem(seq, 2)
    crossed = jnp.logical_and(core == 1, jnp.logical_or(hid > 0, seq >= 2))

    def copy(source, target, index):
        return pltpu.make_async_copy(source, target, semaphores.at[index])

    inputs = [
        copy(received_any, received_ref, 0),
        copy(mirror_any, mirror_ref, 1),
        copy(own_any, own_ref, 2),
        copy(local_any, local_ref, 3),
    ]
    for each in inputs:
        each.start()
    inner_from = [(inner_ref, inner_ref)]
    outer_from = [(outer_ref, outer_ref)]
    small_from = [(payload_ref, payload_ref)]
    for i, j in ((0, 2), (2, 0), (1, 1)):
        pair = (ring_refs[i], swapped_refs[i])
        inner_from.append(tuple(each.at[pl.ds(0, D)] for each in pair))
        small_from.append(pair)
        outer_from.append(
            tuple(each.at[pl.ds(0, D)] for each in (swapped_refs[j], ring_refs[j]))
        )
    sources = [each for pair in zip(inner_from, outer_from) for each in pair]

    def small_copy(which, taken_by):
        source = small_from[which][taken_by].at[pl.ds(D, EXTRA)]
        return copy(source, around_ref.at[(0, 3, 1, 2)[which]], 4 + which)

    for taken_by in range(2):

        @pl.when(core == taken_by)
        def _():
            for which in range(4):
                small_copy(which, taken_by).start()
            for index, each in enumerate(sources):
                copy(each[taken_by], weights_ref.at[index], 8 + index).start()

    inputs += [small_copy(which, 0) for which in range(4)]
    for each in inputs:
        each.wait()
    for block in range(4):
        at = lax.rem(block - hid + 4, 4)
        sums = whole_rows(around_ref[at])
        for index in range(5):
            row, column = divmod(index, 4)
            rows_ref[index : index + 1, pl.ds(block * WIDTH, WIDTH)] = sums[
                row : row + 1, column * WIDTH : (column + 1) * WIDTH
            ]

    received = received_ref[...]
    own = own_ref[...]
    lane = lax.broadcasted_iota(jnp.int32, (R, HALF), 1)
    take = jnp.logical_and(lane == 0, crossed)
    low = jnp.where(take, received.astype(jnp.float32), own)
    high = jnp.where(take, own, dot(received, mirror_ref[...]))
    mixed = jnp.concatenate([low, high], axis=1)
    first_sum = local_ref[...].astype(jnp.float32) + mixed
    normed = norm_rows(first_sum, rows_ref[0:1, :], rows_ref[1:2, :]).astype(jnp.bfloat16)
    total_ref[...] = normed.astype(jnp.float32) + rows_ref[2:3, :]
    def project(index):
        for at in (2 * index, 2 * index + 1):
            copy(sources[at][0], weights_ref.at[at], 8 + at).wait()
        return dot(normed, weights_ref[2 * index])

    later = project(0)
    for index, distance in enumerate((0, 3, 1, 2)):
        inner = later + whole_rows(around_ref[distance])[2:3]
        if index < 3:
            later = project(index + 1)
        active = jax.nn.gelu(inner, approximate=True).astype(jnp.bfloat16)
        total_ref[...] += dot(active, weights_ref[2 * index + 1])
    finished = norm_rows(total_ref[...], rows_ref[3:4, :], rows_ref[4:5, :]).astype(out_ref.dtype)
    for block in range(4):
        for u in range(2):
            folded_ref[pl.ds(block * 128, 128), pl.ds(u * WIDTH, WIDTH)] = finished[
                u * 128 : (u + 1) * 128, block * WIDTH : (block + 1) * WIDTH
            ]
    out_ref[...] = folded_ref[...].reshape(out_ref.shape)


VMEM = pl.BlockSpec(memory_space=pltpu.VMEM)
HBM = pl.BlockSpec(memory_space=pltpu.HBM)
ANYWHERE = pl.BlockSpec(memory_space=pl.ANY)
EXTRA = 32
HIDDEN = pl.CostEstimate(flops=10**10, bytes_accessed=2 * 10**7, transcendentals=0)


def params(mebibytes):
    return pltpu.CompilerParams(vmem_limit_bytes=mebibytes * 2**20)


def array(shape, dtype=jnp.bfloat16):
    return jax.ShapeDtypeStruct(shape, dtype)


def pair_index(seq, hid):
    return seq * HID_DEVICES + hid % HID_DEVICES


def ring(value, sign):
    pairs = []
    for seq in range(SEQ_DEVICES):
        step = -sign if seq & 1 else sign
        for hid in range(HID_DEVICES):
            pairs.append((pair_index(seq, hid), pair_index(seq, hid + step)))
    return lax.ppermute(value, ("seq", "hid"), pairs)


def swap_cores(value):
    return lax.ppermute(value, "seq", [(seq, seq ^ 1) for seq in range(SEQ_DEVICES)])


def swap_mirrored(value):
    pairs = []
    for seq in range(SEQ_DEVICES):
        for hid in range(HID_DEVICES):
            alone = seq < 2 and hid == 0
            pairs.append((pair_index(seq, hid), pair_index(seq if alone else seq ^ 1, hid)))
    return lax.ppermute(value, ("seq", "hid"), pairs)


def shift_hid(value, step):
    pairs = [(hid, (hid + step) % HID_DEVICES) for hid in range(HID_DEVICES)]
    return lax.ppermute(value, "hid", pairs)


def low_matrix(opposed, after):
    table, _ = lax.optimization_barrier((jnp.asarray(LOW_TABLE), after))
    return pl.pallas_call(
        functools.partial(turn_kernel, opposed),
        out_shape=array((R, 2 * R)),
        in_specs=[VMEM],
        out_specs=VMEM,
        compiler_params=params(8),
        cost_estimate=HIDDEN,
    )(table)


def shards(
    tokens,
    first_gain,
    first_shift,
    inner_weight,
    inner_bias,
    outer_weight,
    outer_bias,
    second_gain,
    second_shift,
):
    bf16 = jnp.bfloat16
    f32 = jnp.float32

    payload = pl.pallas_call(
        payload_kernel,
        out_shape=array((D + EXTRA, D)),
        in_specs=[HBM] * 8,
        out_specs=HBM,
        scratch_shapes=[
            pltpu.VMEM((D, D), bf16),
            pltpu.VMEM((EXTRA, D), bf16),
            pltpu.VMEM((8, D), f32),
            *[pltpu.VMEM((WIDTH,), f32)] * 5,
            pltpu.VMEM((D,), f32),
            pltpu.SemaphoreType.DMA((15,)),
        ],
        compiler_params=params(62),
    )(
        inner_weight,
        outer_weight,
        first_gain,
        first_shift,
        outer_bias,
        second_gain,
        second_shift,
        inner_bias,
    )
    ring_one = ring(payload, 1)

    tokens_t, _ = lax.optimization_barrier((tokens.T, payload))
    sent = pl.pallas_call(
        scatter_kernel,
        out_shape=array(CHUNKS),
        in_specs=[VMEM],
        out_specs=VMEM,
        scratch_shapes=[pltpu.VMEM((HALF, 2 * R), bf16)],
        compiler_params=params(8),
    )(tokens_t)
    taken = lax.all_to_all(sent, EVERY, 0, 0, tiled=True)

    own_matrix = low_matrix(False, sent)
    (ring_one, late), _ = lax.optimization_barrier(((ring_one, payload), own_matrix))
    ring_two, ring_three = ring(ring_one, 1), ring(late, -1)
    swap_one = swap_cores(ring_one)
    taken, _ = lax.optimization_barrier((taken, own_matrix))

    local, sent = pl.pallas_call(
        high_kernel,
        out_shape=(array((R, D)), array(CHUNKS)),
        in_specs=[VMEM] * 3,
        out_specs=(HBM, VMEM),
        scratch_shapes=[
            pltpu.VMEM((R, D), bf16),
            pltpu.VMEM((2 * R, 2 * R), bf16),
            pltpu.SemaphoreType.DMA,
        ],
        compiler_params=params(16),
    )(taken, jnp.asarray(FEATURE), jnp.asarray(HIGH_TABLE))
    taken = lax.all_to_all(sent, EVERY, 0, 0, tiled=True)

    other_matrix = low_matrix(True, sent)
    (ring_two, ring_three), _ = lax.optimization_barrier(((ring_two, ring_three), other_matrix))
    swap_two, swap_three = swap_cores(ring_two), swap_cores(ring_three)

    own, other = pl.pallas_call(
        low_kernel,
        out_shape=(array((R, HALF), f32), array((R, HALF))),
        in_specs=[VMEM] * 3,
        out_specs=(VMEM, VMEM),
        scratch_shapes=[pltpu.VMEM((2 * R, 2 * R), bf16)],
        compiler_params=params(8),
        cost_estimate=HIDDEN,
    )(taken, own_matrix, other_matrix)
    received = swap_mirrored(other)

    def layer(*refs):
        return layer_kernel(*refs[:7], refs[7:10], refs[10:13], *refs[13:])

    sent = pl.pallas_call(
        layer,
        out_shape=array(CHUNKS),
        in_specs=[ANYWHERE] * 2 + [HBM] * 2 + [ANYWHERE] * 9,
        out_specs=VMEM,
        scratch_shapes=[
            pltpu.VMEM((R, HALF), f32),
            pltpu.VMEM((R, HALF), bf16),
            pltpu.VMEM((HALF, HALF), bf16),
            pltpu.VMEM((R, D), bf16),
            pltpu.VMEM((4, EXTRA, D), bf16),
            pltpu.VMEM((8, D, D), bf16),
            pltpu.VMEM((8, D), f32),
            pltpu.VMEM((R, D), f32),
            pltpu.VMEM((2 * R, HALF), bf16),
            pltpu.SemaphoreType.DMA((16,)),
        ],
        compiler_params=params(52),
    )(
        own,
        received,
        jnp.asarray(MIRROR),
        local,
        inner_weight,
        outer_weight,
        payload,
        ring_one,
        ring_two,
        ring_three,
        swap_one,
        swap_two,
        swap_three,
    )
    taken = lax.all_to_all(sent, EVERY, 0, 0, tiled=True)

    return pl.pallas_call(
        gather_kernel,
        out_shape=array(tokens.shape[::-1]),
        in_specs=[VMEM],
        out_specs=VMEM,
        compiler_params=params(8),
    )(taken).T


def solution(mesh):
    return jax.shard_map(
        shards,
        mesh=mesh,
        in_specs=(
            P("seq", "hid"),
            P("hid"),
            P("hid"),
            P(None, "hid"),
            P("hid"),
            P("hid", None),
            P("hid"),
            P("hid"),
            P("hid"),
        ),
        out_specs=P("seq", "hid"),
        check_vma=False,
    )
```

```python
import functools
import math

import jax
import jax.numpy as jnp
import ml_dtypes
import numpy as np
from jax import lax
from jax.experimental import pallas as pl
from jax.experimental.pallas import tpu as pltpu
from jax.sharding import PartitionSpec as P

D = 768
HALF = D // 2
SEQ = 65536
R = 256
SEQ_DEVICES = 64
HID_DEVICES = 4
WIDTH = D // HID_DEVICES
EVERY = ("hid", "seq")
CHUNKS = (R, 2, HALF)
BF16 = ml_dtypes.bfloat16


def residues():
    place = np.arange(R)
    hid, seq = place // SEQ_DEVICES, place % SEQ_DEVICES
    chip = (seq >> 1) * HID_DEVICES + hid
    core = seq & 1
    return np.where(core == 0, chip, np.where(chip == 0, R // 2, R - chip)), chip, core


RESIDUE, CHIP, CORE = residues()
ROW = np.arange(R)
HIGH = 4 * (ROW % 128 // 2) + 2 * (ROW % 2) + ROW // 128


def cosine_sine(phase, period):
    angle = 2.0 * np.pi * (phase % period).astype(np.float64) / period
    return np.cos(angle), np.sin(angle)


def feature_table():
    rows = np.arange(D, dtype=np.int64)[:, None]
    columns = np.arange(HALF + 1, dtype=np.int64)[None, :]
    angle = np.float32(2.0 * math.pi / D) * (rows * columns % D).astype(np.float32)
    cosine = np.cos(angle.astype(np.float64)).astype(BF16)
    sine = (-np.sin(angle.astype(np.float64))).astype(BF16)
    sine[:, 0] = cosine[:, HALF]
    return np.concatenate([cosine[:, :HALF], sine[:, :HALF]], axis=1)


def pairs_of_rows(even, odd):
    return np.stack([even, odd], axis=1).reshape(2 * even.shape[0], -1)


def high_table():
    cosine, sine = cosine_sine(RESIDUE[:, None] * HIGH[None, :], R)
    even = np.concatenate([cosine, sine], axis=1)
    odd = np.concatenate([-sine, cosine], axis=1)
    return pairs_of_rows(even, odd).astype(BF16)


def low_table():
    cosine, sine = cosine_sine(HIGH[:, None] * RESIDUE[None, :], R)
    table = np.stack([pairs_of_rows(cosine.T, sine.T).T, pairs_of_rows(-sine.T, cosine.T).T])
    return table.astype(np.float32)


FEATURE = feature_table()
HIGH_TABLE = high_table()
LOW_TABLE = low_table()
LANE = np.arange(HALF)
MIRROR = (LANE[:, None] == (HALF - LANE[None, :]) % HALF).astype(BF16)


def dot(left, right):
    return jnp.dot(left, right, preferred_element_type=jnp.float32)


def norm_rows(values, gain, shift):
    mean = jnp.mean(values, axis=1, keepdims=True)
    spread = jnp.mean(values * values, axis=1, keepdims=True) - mean * mean
    return (values - mean) * lax.rsqrt(spread + 1e-05) * gain + shift


def residue_of(place):
    hid, seq = place // SEQ_DEVICES, place % SEQ_DEVICES
    chip = seq // 2 * HID_DEVICES + hid
    late = jnp.where(chip == 0, R // 2, R - chip)
    return jnp.where(seq % 2 == 0, chip, late)


def spread_matrix():
    pair = lax.broadcasted_iota(jnp.int32, (2 * R, 1), 0)
    target = pair % 2 * R + residue_of(pair // 2)
    column = lax.broadcasted_iota(jnp.int32, (1, 2 * R), 1)
    return jnp.where(target == column, 1.0, 0.0).astype(jnp.bfloat16)


def payload_kernel(inner_ref, outer_ref, *rest):
    sources, rest = rest[:6], rest[6:]
    payload_ref, held_ref, parts_ref, rows_ref, *vector_refs, semaphores = rest
    vectors = [
        pltpu.make_async_copy(source, target, semaphores.at[9 + at])
        for at, (source, target) in enumerate(zip(sources, vector_refs))
    ]
    for each in vectors:
        each.start()
    core = lax.rem(lax.axis_index("seq"), 2)
    pieces_of_rows = [pl.ds(at * WIDTH, WIDTH) for at in range(4)]

    def fetch(source, at):
        rows = pieces_of_rows[at]
        return pltpu.make_async_copy(source.at[rows], held_ref.at[rows], semaphores.at[at])

    @pl.when(core == 0)
    def _():
        for at in range(4):
            fetch(inner_ref, at).start()

    @pl.when(core == 1)
    def _():
        for at in range(4):
            fetch(outer_ref, at).start()

    for each in vectors:
        each.wait()
    rows_ref[...] = jnp.zeros_like(rows_ref)
    for index, each in enumerate(vector_refs):
        row, at = divmod(index, 4) if index < 5 else (2, 0)
        rows_ref[row : row + 1, pl.ds(at * WIDTH, each.shape[0])] = each[...][None, :]
    rest = rows_ref[...]
    pieces = []
    for _ in range(3):
        pieces.append(rest.astype(jnp.bfloat16).astype(jnp.float32))
        rest = rest - pieces[-1]
    pieces.append(jnp.zeros_like(rest))
    parts_ref[...] = jnp.concatenate(pieces, axis=0).astype(jnp.bfloat16)
    copies = [pltpu.make_async_copy(parts_ref, payload_ref.at[pl.ds(D, EXTRA)], semaphores.at[8])]
    copies[0].start()
    for at, rows in enumerate(pieces_of_rows):
        fetch(inner_ref, at).wait()
        copies.append(
            pltpu.make_async_copy(held_ref.at[rows], payload_ref.at[rows], semaphores.at[4 + at])
        )
        copies[-1].start()
    for each in copies:
        each.wait()


def scatter_kernel(tokens_ref, out_ref, wide_ref):
    for a in range(4):
        s, u = divmod(a, 2)
        wide_ref[pl.ds(u * WIDTH, WIDTH), pl.ds(s * R, R)] = tokens_ref[:, pl.ds(a * R, R)]
    spread = lax.dot_general(
        spread_matrix(),
        wide_ref[...],
        (((1,), (1,)), ((), ())),
        preferred_element_type=jnp.float32,
    )
    out_ref[...] = spread.astype(out_ref.dtype).reshape(out_ref.shape)


def gather_kernel(taken_ref, out_ref):
    ordered = lax.dot_general(
        taken_ref[...].reshape(2 * R, HALF),
        spread_matrix(),
        (((0,), (0,)), ((), ())),
        preferred_element_type=jnp.float32,
    ).astype(out_ref.dtype)
    for a in range(4):
        s, u = divmod(a, 2)
        out_ref[:, pl.ds(a * R, R)] = ordered[u * WIDTH : (u + 1) * WIDTH, s * R : (s + 1) * R]


def high_kernel(taken_ref, feature_ref, table_ref, kept_ref, out_ref, local_ref, stacked_ref, semaphore):
    taken = taken_ref[...].reshape(2 * R, HALF)
    for hid in range(4):
        for u in range(2):
            local_ref[pl.ds(u * 128, 128), pl.ds(hid * WIDTH, WIDTH)] = taken[
                hid * 128 : (hid + 1) * 128, u * WIDTH : (u + 1) * WIDTH
            ]
    keep = pltpu.make_async_copy(local_ref, kept_ref, semaphore)
    keep.start()
    features = dot(local_ref[...], feature_ref[...])
    stacked_ref[pl.ds(0, R), pl.ds(0, HALF)] = features[:, :HALF].astype(jnp.bfloat16)
    stacked_ref[pl.ds(R, R), pl.ds(0, HALF)] = features[:, HALF:].astype(jnp.bfloat16)
    lane = lax.broadcasted_iota(jnp.int32, (R, 128), 1)
    first, middle = features[:, 0:1], features[:, HALF : HALF + 1]
    above = jnp.where(lane == 0, first, jnp.where(lane == 1, middle, 0.0))
    below = jnp.where(lane == 2, middle, 0.0)
    stacked_ref[pl.ds(0, R), pl.ds(HALF, 128)] = above.astype(jnp.bfloat16)
    stacked_ref[pl.ds(R, R), pl.ds(HALF, 128)] = below.astype(jnp.bfloat16)
    turned = dot(table_ref[...], stacked_ref[...])
    pair = lax.broadcasted_iota(jnp.int32, (2 * R, 128), 0)
    lane = lax.broadcasted_iota(jnp.int32, (2 * R, 128), 1)
    there = pair // 2
    alone = there < 2
    edge = turned[:, HALF:]
    single = jnp.where(jnp.logical_and(alone, pair % 2 == 1), edge[:, 2:3], edge[:, 0:1])
    single = jnp.where(jnp.logical_and(~alone, there % 2 == 1), edge[:, 1:2], single)
    head = jnp.where(lane == 0, single, turned[:, :128])
    sent = jnp.concatenate([head, turned[:, 128:HALF]], axis=1)
    out_ref[...] = sent.astype(out_ref.dtype).reshape(out_ref.shape)
    keep.wait()


def turn_kernel(opposed, table_ref, out_ref):
    residue = residue_of(lax.axis_index("hid") * SEQ_DEVICES + lax.axis_index("seq"))
    column = lax.broadcasted_iota(jnp.int32, (8, 2 * R), 1)
    opposite = jnp.where(residue == 0, 0, R - residue)
    row = lax.broadcasted_iota(jnp.int32, (8, 2 * R), 0)
    phase = jnp.where(row == 0, residue, opposite) * residue_of(column // 2)
    angle = phase.astype(jnp.float32) * (2.0 * math.pi / SEQ)
    sign = jnp.where(jnp.logical_or(row == 0, column % 2 == 0), 1.0, -1.0)
    cosine, sine = jnp.cos(angle) * sign, jnp.sin(angle) * sign
    index = int(opposed)
    matrix = table_ref[0] * cosine[index : index + 1] + table_ref[1] * sine[index : index + 1]
    out_ref[...] = matrix.astype(out_ref.dtype)


def low_kernel(taken_ref, first_ref, second_ref, own_ref, other_ref, wide_ref):
    scale = 1.0 / math.sqrt(SEQ * D)
    alone = jnp.logical_and(lax.axis_index("hid") == 0, lax.axis_index("seq") < 2)
    taken = taken_ref[...].reshape(2 * R, HALF)
    wide_ref[:, pl.ds(0, HALF)] = taken
    edge = taken[:, :128].astype(jnp.float32)
    row = lax.broadcasted_iota(jnp.int32, (2 * R, 128), 0)
    lane = lax.broadcasted_iota(jnp.int32, (2 * R, 128), 1)
    raised = pltpu.roll(pltpu.roll(edge, 2 * R - 1, 0), 1, 1)
    edge = jnp.where(row % 2 == 0, jnp.where(lane == 0, edge, raised), 0.0)
    wide_ref[:, pl.ds(HALF, 128)] = edge.astype(wide_ref.dtype)
    lane = lax.broadcasted_iota(jnp.int32, (R, 128), 1)
    single = jnp.logical_and(lane == 0, alone)
    for index, (matrix_ref, out_ref) in enumerate(((first_ref, own_ref), (second_ref, other_ref))):
        usual = dot(matrix_ref[...], wide_ref[...]) * scale
        edge = usual[:, HALF + index : HALF + index + 1]
        out_ref[:, pl.ds(0, 128)] = jnp.where(single, edge, usual[:, :128]).astype(out_ref.dtype)
        out_ref[:, pl.ds(128, HALF - 128)] = usual[:, 128:HALF].astype(out_ref.dtype)


def whole_rows(parts):
    parts = parts.astype(jnp.float32)
    return parts[0:8] + parts[8:16] + parts[16:24]


def layer_kernel(
    own_any,
    received_any,
    mirror_any,
    local_any,
    inner_ref,
    outer_ref,
    payload_ref,
    ring_refs,
    swapped_refs,
    out_ref,
    own_ref,
    received_ref,
    mirror_ref,
    local_ref,
    around_ref,
    weights_ref,
    rows_ref,
    total_ref,
    active_ref,
    folded_ref,
    semaphores,
):
    hid, seq = lax.axis_index("hid"), lax.axis_index("seq")
    core = lax.rem(seq, 2)
    crossed = jnp.logical_and(core == 1, jnp.logical_or(hid > 0, seq >= 2))

    def copy(source, target, index):
        return pltpu.make_async_copy(source, target, semaphores.at[index])

    inputs = [
        copy(received_any, received_ref, 0),
        copy(mirror_any, mirror_ref, 1),
        copy(own_any, own_ref, 2),
        copy(local_any, local_ref, 3),
    ]
    for each in inputs:
        each.start()
    inner_from = [(inner_ref, inner_ref)]
    outer_from = [(outer_ref, outer_ref)]
    small_from = [(payload_ref, payload_ref)]
    for i, j in ((0, 2), (2, 0), (1, 1)):
        pair = (ring_refs[i], swapped_refs[i])
        inner_from.append(tuple(each.at[pl.ds(0, D)] for each in pair))
        small_from.append(pair)
        outer_from.append(
            tuple(each.at[pl.ds(0, D)] for each in (swapped_refs[j], ring_refs[j]))
        )
    sources = inner_from + outer_from

    def small_copy(which, taken_by):
        source = small_from[which][taken_by].at[pl.ds(D, EXTRA)]
        return copy(source, around_ref.at[(0, 3, 1, 2)[which]], 4 + which)

    for taken_by in range(2):

        @pl.when(core == taken_by)
        def _():
            for which in range(4):
                small_copy(which, taken_by).start()
            for index, each in enumerate(sources):
                copy(each[taken_by], weights_ref.at[index], 8 + index).start()

    inputs += [small_copy(which, 0) for which in range(4)]
    for each in inputs:
        each.wait()
    for block in range(4):
        at = lax.rem(block - hid + 4, 4)
        sums = whole_rows(around_ref[at])
        for index in range(5):
            row, column = divmod(index, 4)
            rows_ref[index : index + 1, pl.ds(block * WIDTH, WIDTH)] = sums[
                row : row + 1, column * WIDTH : (column + 1) * WIDTH
            ]

    received = received_ref[...]
    own = own_ref[...]
    lane = lax.broadcasted_iota(jnp.int32, (R, HALF), 1)
    take = jnp.logical_and(lane == 0, crossed)
    low = jnp.where(take, received.astype(jnp.float32), own)
    high = jnp.where(take, own, dot(received, mirror_ref[...]))
    mixed = jnp.concatenate([low, high], axis=1)
    first_sum = local_ref[...].astype(jnp.float32) + mixed
    normed = norm_rows(first_sum, rows_ref[0:1, :], rows_ref[1:2, :]).astype(jnp.bfloat16)
    total_ref[...] = normed.astype(jnp.float32) + rows_ref[2:3, :]
    def project(index):
        copy(sources[index][0], weights_ref.at[index], 8 + index).wait()
        return dot(normed, weights_ref[index])

    later = project(0)
    for index, distance in enumerate((0, 3, 1, 2)):
        inner = later + whole_rows(around_ref[distance])[2:3]
        if index < 3:
            later = project(index + 1)
        active_ref[:, pl.ds(index * D, D)] = jax.nn.gelu(inner, approximate=True).astype(
            jnp.bfloat16
        )
    for at in range(4, 8):
        copy(sources[at][0], weights_ref.at[at], 8 + at).wait()
    total_ref[...] += dot(active_ref[...], weights_ref[4:8].reshape(4 * D, D))
    finished = norm_rows(total_ref[...], rows_ref[3:4, :], rows_ref[4:5, :]).astype(out_ref.dtype)
    for block in range(4):
        for u in range(2):
            folded_ref[pl.ds(block * 128, 128), pl.ds(u * WIDTH, WIDTH)] = finished[
                u * 128 : (u + 1) * 128, block * WIDTH : (block + 1) * WIDTH
            ]
    out_ref[...] = folded_ref[...].reshape(out_ref.shape)


VMEM = pl.BlockSpec(memory_space=pltpu.VMEM)
HBM = pl.BlockSpec(memory_space=pltpu.HBM)
ANYWHERE = pl.BlockSpec(memory_space=pl.ANY)
EXTRA = 32
HIDDEN = pl.CostEstimate(flops=10**10, bytes_accessed=2 * 10**7, transcendentals=0)


def params(mebibytes):
    return pltpu.CompilerParams(vmem_limit_bytes=mebibytes * 2**20)


def array(shape, dtype=jnp.bfloat16):
    return jax.ShapeDtypeStruct(shape, dtype)


def pair_index(seq, hid):
    return seq * HID_DEVICES + hid % HID_DEVICES


def ring(value, sign):
    pairs = []
    for seq in range(SEQ_DEVICES):
        step = -sign if seq & 1 else sign
        for hid in range(HID_DEVICES):
            pairs.append((pair_index(seq, hid), pair_index(seq, hid + step)))
    return lax.ppermute(value, ("seq", "hid"), pairs)


def swap_cores(value):
    return lax.ppermute(value, "seq", [(seq, seq ^ 1) for seq in range(SEQ_DEVICES)])


def swap_mirrored(value):
    pairs = []
    for seq in range(SEQ_DEVICES):
        for hid in range(HID_DEVICES):
            alone = seq < 2 and hid == 0
            pairs.append((pair_index(seq, hid), pair_index(seq if alone else seq ^ 1, hid)))
    return lax.ppermute(value, ("seq", "hid"), pairs)


def shift_hid(value, step):
    pairs = [(hid, (hid + step) % HID_DEVICES) for hid in range(HID_DEVICES)]
    return lax.ppermute(value, "hid", pairs)


def low_matrix(opposed, after):
    table, _ = lax.optimization_barrier((jnp.asarray(LOW_TABLE), after))
    return pl.pallas_call(
        functools.partial(turn_kernel, opposed),
        out_shape=array((R, 2 * R)),
        in_specs=[VMEM],
        out_specs=VMEM,
        compiler_params=params(8),
        cost_estimate=HIDDEN,
    )(table)


def shards(
    tokens,
    first_gain,
    first_shift,
    inner_weight,
    inner_bias,
    outer_weight,
    outer_bias,
    second_gain,
    second_shift,
):
    bf16 = jnp.bfloat16
    f32 = jnp.float32

    payload = pl.pallas_call(
        payload_kernel,
        out_shape=array((D + EXTRA, D)),
        in_specs=[HBM] * 8,
        out_specs=HBM,
        scratch_shapes=[
            pltpu.VMEM((D, D), bf16),
            pltpu.VMEM((EXTRA, D), bf16),
            pltpu.VMEM((8, D), f32),
            *[pltpu.VMEM((WIDTH,), f32)] * 5,
            pltpu.VMEM((D,), f32),
            pltpu.SemaphoreType.DMA((15,)),
        ],
        compiler_params=params(62),
    )(
        inner_weight,
        outer_weight,
        first_gain,
        first_shift,
        outer_bias,
        second_gain,
        second_shift,
        inner_bias,
    )
    ring_one = ring(payload, 1)

    tokens_t, _ = lax.optimization_barrier((tokens.T, payload))
    sent = pl.pallas_call(
        scatter_kernel,
        out_shape=array(CHUNKS),
        in_specs=[VMEM],
        out_specs=VMEM,
        scratch_shapes=[pltpu.VMEM((HALF, 2 * R), bf16)],
        compiler_params=params(8),
    )(tokens_t)
    taken = lax.all_to_all(sent, EVERY, 0, 0, tiled=True)

    own_matrix = low_matrix(False, sent)
    (ring_one, late), _ = lax.optimization_barrier(((ring_one, payload), own_matrix))
    ring_two, ring_three = ring(ring_one, 1), ring(late, -1)
    swap_one = swap_cores(ring_one)
    taken, _ = lax.optimization_barrier((taken, own_matrix))

    local, sent = pl.pallas_call(
        high_kernel,
        out_shape=(array((R, D)), array(CHUNKS)),
        in_specs=[VMEM] * 3,
        out_specs=(HBM, VMEM),
        scratch_shapes=[
            pltpu.VMEM((R, D), bf16),
            pltpu.VMEM((2 * R, 2 * R), bf16),
            pltpu.SemaphoreType.DMA,
        ],
        compiler_params=params(16),
    )(taken, jnp.asarray(FEATURE), jnp.asarray(HIGH_TABLE))
    taken = lax.all_to_all(sent, EVERY, 0, 0, tiled=True)

    other_matrix = low_matrix(True, sent)
    (ring_two, ring_three), _ = lax.optimization_barrier(((ring_two, ring_three), other_matrix))
    swap_two, swap_three = swap_cores(ring_two), swap_cores(ring_three)

    own, other = pl.pallas_call(
        low_kernel,
        out_shape=(array((R, HALF), f32), array((R, HALF))),
        in_specs=[VMEM] * 3,
        out_specs=(VMEM, VMEM),
        scratch_shapes=[pltpu.VMEM((2 * R, 2 * R), bf16)],
        compiler_params=params(8),
        cost_estimate=HIDDEN,
    )(taken, own_matrix, other_matrix)
    received = swap_mirrored(other)

    def layer(*refs):
        return layer_kernel(*refs[:7], refs[7:10], refs[10:13], *refs[13:])

    sent = pl.pallas_call(
        layer,
        out_shape=array(CHUNKS),
        in_specs=[ANYWHERE] * 2 + [HBM] * 2 + [ANYWHERE] * 9,
        out_specs=VMEM,
        scratch_shapes=[
            pltpu.VMEM((R, HALF), f32),
            pltpu.VMEM((R, HALF), bf16),
            pltpu.VMEM((HALF, HALF), bf16),
            pltpu.VMEM((R, D), bf16),
            pltpu.VMEM((4, EXTRA, D), bf16),
            pltpu.VMEM((8, D, D), bf16),
            pltpu.VMEM((8, D), f32),
            pltpu.VMEM((R, D), f32),
            pltpu.VMEM((R, 4 * D), bf16),
            pltpu.VMEM((2 * R, HALF), bf16),
            pltpu.SemaphoreType.DMA((16,)),
        ],
        compiler_params=params(52),
    )(
        own,
        received,
        jnp.asarray(MIRROR),
        local,
        inner_weight,
        outer_weight,
        payload,
        ring_one,
        ring_two,
        ring_three,
        swap_one,
        swap_two,
        swap_three,
    )
    taken = lax.all_to_all(sent, EVERY, 0, 0, tiled=True)

    return pl.pallas_call(
        gather_kernel,
        out_shape=array(tokens.shape[::-1]),
        in_specs=[VMEM],
        out_specs=VMEM,
        compiler_params=params(8),
    )(taken).T


def solution(mesh):
    return jax.shard_map(
        shards,
        mesh=mesh,
        in_specs=(
            P("seq", "hid"),
            P("hid"),
            P("hid"),
            P(None, "hid"),
            P("hid"),
            P("hid", None),
            P("hid"),
            P("hid"),
            P("hid"),
        ),
        out_specs=P("seq", "hid"),
        check_vma=False,
    )
```
